256 devices in a mesh: dp: 32 (over y, z), tensor: 8 (over x, core).
Axes of the slice: x: 4, y: 4, z: 8, core: 2. Of those that a mesh axis runs over, the one named last changes fastest.
Arguments:
- queries: bfloat16 [8192, 8192], P('dp', 'tensor')
- keys: bfloat16 [8192, 1024], P('dp', 'tensor')
- values: bfloat16 [8192, 1024], P('dp', 'tensor'), may hold values from -6 to 6
- prompt_keys: bfloat16 [4096, 1024], P('dp', 'tensor'), may hold values from -6 to 6
- prompt_values: bfloat16 [4096, 1024], P('dp', 'tensor'), may hold values from -6 to 6
- lengths: int32 [32, 4], P('dp'), may hold values from 1 to 128, 256 in all within a row
- owner_slice: int32 [32], replicated, may hold values from 0 to 31, each once
- device_group: int32 [32], replicated, may hold values from 0 to 7
- out_weight: bfloat16 [8192, 5120], P('tensor'), may hold values from -0.0625 to 0.0625
- cotangent: bfloat16 [8192, 5120], P('dp', 'tensor'), may hold values from -6 to 6
Outputs:
- block_out: bfloat16 [8192, 5120], P(('dp', 'tensor'))
- grad_queries: bfloat16 [8192, 8192], P('dp', 'tensor')
- grad_keys: bfloat16 [8192, 1024], P('dp', 'tensor')
- grad_values: bfloat16 [8192, 1024], P('dp', 'tensor')
- grad_prompt_keys: float32 [4096, 1024], P('dp', 'tensor')
- grad_prompt_values: float32 [4096, 1024], P('dp', 'tensor')
The draws below stay inside these ranges and needn't reach their ends.
Inputs may be any that keep to these rules, and one draw needn't show every extreme that they name: Each row holds 4 lengths that sum to 256; its largest is exactly half of 256. `owner_slice`: a permutation of the 32 prompt slices.
All inputs are finite; a program needn't handle non-finite values.
Results may differ from the reference program's by a relative error of at most 0.034.
Values may be sent and summed in bfloat16 or wider, within the bound.
A program may use at most 128 MiB of HBM per device.

```python
import math
import jax
import jax.numpy as jnp
import numpy as np
from jax import lax

D = 5120
HEADS = 64
KV_HEADS = 8
HEAD = 128
RESP_ROWS = 256
RESP = 4
PROMPT = 512
PIECES = 4
SLICE = 128
GROUPS = 8
TOKENS = 8192
N_DP = 32


def shared_keys(key):
    return jax.random.normal(key, (TOKENS, KV_HEADS * HEAD), jnp.float32)


def draw_keys(key, part):
    base = shared_keys(key)
    return base.astype(jnp.bfloat16)


def draw_queries(key, part):
    key = jax.random.fold_in(key, 7)
    drawn = jax.random.normal(key, (TOKENS, HEADS * HEAD), jnp.float32)
    return drawn.astype(jnp.bfloat16)


def set_ends(drawn, own_key, low, top_value):
    shape = drawn.shape
    index_at = [jax.random.randint(jax.random.fold_in(own_key, axis), (), 0, shape[axis]) for axis in range(len(shape))]
    drawn = drawn.at[tuple(index_at)].set(low)
    longest = shape.index(max(shape))
    index_at[longest] = (index_at[longest] + 1) % shape[longest]
    return drawn.at[tuple(index_at)].set(top_value)


def levels(rng, extent, pieces, least, largest):
    factor_of, own = 1.0, jax.random.fold_in(rng, 6)
    for dim, parts in pieces:
        draws = jnp.exp(jax.random.uniform(jax.random.fold_in(own, dim), (parts,), jnp.float32, least / len(pieces), largest / len(pieces)))
        factor_of = factor_of * jnp.repeat(draws, extent[dim] // parts).reshape([-1 if axis == dim else 1 for axis in range(len(extent))])
    return factor_of


def profile(amount, total, limit, slope):
    loads = [(1 << 20) // math.isqrt(standing ** slope) + 1 for standing in range(2, amount + 1)]
    surplus, holding = total - limit - (amount - 1), [1] * (amount - 1)
    while surplus > 0:
        candidates = [i for i in range(amount - 1) if holding[i] < limit]
        whole, left = sum([loads[i] for i in candidates]), surplus
        for i in candidates:
            addition = min(limit - holding[i], max(1, left * loads[i] // whole), surplus)
            holding[i] = holding[i] + addition
            surplus = surplus - addition
    return np.array([limit] + holding)


def ragged(own_key, number_of, total, bound, lean):
    if number_of == 2:
        one = jax.random.randint(own_key, (), max(1, total - bound), min(bound, total - 1) + 1)
        return jnp.stack([one, total - one])
    tallies = jnp.asarray(profile(number_of, total, bound, lean), jnp.int32)
    couples = (number_of - 1) // 2
    source_of, receiver = tallies[1:1 + 2 * couples:2], tallies[2:2 + 2 * couples:2]
    margin = jnp.minimum(source_of - 1, bound - receiver)
    passed = jax.random.randint(jax.random.fold_in(own_key, 1), (couples,), 0, 1 << 20) % (margin + 1)
    tallies = tallies.at[1:1 + 2 * couples:2].set(source_of - passed).at[2:2 + 2 * couples:2].set(receiver + passed)
    return tallies[jax.random.permutation(jax.random.fold_in(own_key, 2), number_of)]


def bell_draw(key, dims, scale, most, shards=(), held_as=jnp.bfloat16):
    entries = scale * jax.random.normal(key, dims, jnp.float32)
    if shards:
        entries = entries * levels(key, dims, shards, -0.22, 0.18)
    return jnp.clip(entries, -most, most).astype(held_as)


def setup_inputs(seed: int = 0) -> dict:
    key_of = jax.random.split(jax.random.key(seed), 11)
    return {
        "queries": draw_queries(jax.random.fold_in(key_of[10], 71), 0),
        "keys": draw_keys(jax.random.fold_in(key_of[10], 71), 0),
        "values": bell_draw(key_of[2], (TOKENS, KV_HEADS * HEAD), 1.0, 6.0, ((0, 32), (1, 8))),
        "prompt_keys": bell_draw(key_of[3], (N_DP * SLICE, KV_HEADS * HEAD), 1.0, 6.0, ((0, 32), (1, 8))),
        "prompt_values": bell_draw(key_of[4], (N_DP * SLICE, KV_HEADS * HEAD), 1.0, 6.0, ((0, 32), (1, 8))),
        "lengths": jax.vmap(lambda own: ragged(own, RESP, RESP_ROWS, RESP_ROWS // 2, 2))(jax.random.split(key_of[5], N_DP)).reshape((N_DP, RESP)).astype(jnp.int32),
        "owner_slice": jax.random.permutation(key_of[6], N_DP).astype(jnp.int32),
        "device_group": set_ends(jax.random.randint(key_of[7], (N_DP,), 0, GROUPS), jax.random.fold_in(key_of[7], 1), 0, GROUPS - 1).astype(jnp.int32),
        "out_weight": bell_draw(key_of[8], (HEADS * HEAD, D), (HEADS * HEAD) ** -0.5, 0.0625, ((0, 8),)),
        "cotangent": bell_draw(key_of[9], (TOKENS, D), 1.0, 6.0, ((0, 32), (1, 8))),
    }


def attention_layer(q, k, v, pk, pv, lens, weight, grad_out):
    rows = q.shape[0]
    ratio = HEADS // KV_HEADS
    scale = HEAD ** -0.5
    qh = q.astype(jnp.float32).reshape(rows, KV_HEADS, ratio, HEAD)
    kh = jnp.concatenate([pk, k], 0).astype(jnp.float32).reshape(PROMPT + rows, KV_HEADS, HEAD)
    vh = jnp.concatenate([pv, v], 0).astype(jnp.float32).reshape(PROMPT + rows, KV_HEADS, HEAD)
    ends = jnp.cumsum(lens).astype(jnp.int32)
    position = jnp.arange(rows, dtype=jnp.int32)
    segment = jnp.sum((position[:, None] >= ends[None, :]).astype(jnp.int32), 1)
    inside = (segment[:, None] == segment[None, :]) & (position[None, :] <= position[:, None])
    mask = jnp.concatenate([jnp.ones((rows, PROMPT), bool), inside], 1)
    scores = jnp.einsum('rkgd,nkd->kgrn', qh, kh) * scale
    scores = jnp.where(mask[None, None], scores, jnp.float32(-1e30))
    top = jnp.max(scores, -1, keepdims=True)
    expo = jnp.exp(scores - top)
    probs = expo / jnp.sum(expo, -1, keepdims=True)
    probs_low = probs.astype(jnp.bfloat16).astype(jnp.float32)
    attended = jnp.einsum('kgrn,nkd->rkgd', probs_low, vh).astype(jnp.bfloat16).reshape(rows, HEADS * HEAD)
    block_out = jnp.dot(attended, weight, preferred_element_type=jnp.float32).astype(jnp.bfloat16)
    grad_att = jnp.dot(grad_out, weight.T, preferred_element_type=jnp.float32).astype(jnp.bfloat16)
    doh = grad_att.astype(jnp.float32).reshape(rows, KV_HEADS, ratio, HEAD)
    oh = attended.astype(jnp.float32).reshape(rows, KV_HEADS, ratio, HEAD)
    delta = jnp.transpose(jnp.sum(doh * oh, -1), (1, 2, 0))
    grad_probs = jnp.einsum('rkgd,nkd->kgrn', doh, vh)
    grad_scores = (probs * (grad_probs - delta[..., None])).astype(jnp.bfloat16).astype(jnp.float32)
    grad_q = (jnp.einsum('kgrn,nkd->rkgd', grad_scores, kh) * scale).astype(jnp.bfloat16).reshape(rows, HEADS * HEAD)
    grad_k = (jnp.einsum('kgrn,rkgd->nkd', grad_scores, qh) * scale).reshape(PROMPT + rows, KV_HEADS * HEAD)
    grad_v = jnp.einsum('kgrn,rkgd->nkd', probs_low, doh).reshape(PROMPT + rows, KV_HEADS * HEAD)
    return (block_out, grad_q, grad_k[PROMPT:].astype(jnp.bfloat16), grad_v[PROMPT:].astype(jnp.bfloat16),
            grad_k[:PROMPT], grad_v[:PROMPT])


def reference(queries, keys, values, prompt_keys, prompt_values, lengths, owner_slice, device_group, out_weight, cotangent):
    width = KV_HEADS * HEAD
    inverse = jnp.zeros((N_DP,), jnp.int32).at[owner_slice].set(jnp.arange(N_DP, dtype=jnp.int32))
    group_keys = prompt_keys.reshape(N_DP, SLICE, width)[inverse].reshape(GROUPS, PIECES * SLICE, width)
    group_values = prompt_values.reshape(N_DP, SLICE, width)[inverse].reshape(GROUPS, PIECES * SLICE, width)

    def step(carry, inputs):
        q, k, v, lens, group, grad_out = inputs
        result = attention_layer(q, k, v, group_keys[group], group_values[group], lens, out_weight, grad_out)
        carry = (carry[0].at[group].add(result[4]), carry[1].at[group].add(result[5]))
        return carry, result[:4]

    start = (jnp.zeros((GROUPS, PROMPT, width), jnp.float32), jnp.zeros((GROUPS, PROMPT, width), jnp.float32))
    inputs = (queries.reshape(N_DP, RESP_ROWS, HEADS * HEAD), keys.reshape(N_DP, RESP_ROWS, width),
              values.reshape(N_DP, RESP_ROWS, width), lengths, device_group,
              cotangent.reshape(N_DP, RESP_ROWS, D))
    carry, outs = lax.scan(step, start, inputs)
    grad_pk = carry[0].reshape(N_DP, SLICE, width)[owner_slice].reshape(N_DP * SLICE, width)
    grad_pv = carry[1].reshape(N_DP, SLICE, width)[owner_slice].reshape(N_DP * SLICE, width)
    return (outs[0].reshape(TOKENS, D), outs[1].reshape(TOKENS, HEADS * HEAD), outs[2].reshape(TOKENS, width),
            outs[3].reshape(TOKENS, width), grad_pk, grad_pv)
```

```python
import functools

import jax
import jax.numpy as jnp
from jax import lax
from jax.experimental import pallas as pl
from jax.experimental.pallas import tpu as pltpu
from jax.sharding import PartitionSpec as P

Y, Z, X = 4, 8, 4
HEAD = 128
HEADS = 8
ROWS = 256
PROMPT = 512
KEYS = PROMPT + ROWS
D = 5120
BLK = D // 8
PAIR = 2 * BLK
CH = 4
CW = D // CH
SUB = 256
SCALE = HEAD**-0.5
EXP_SCALE = SCALE * 1.4426950408889634
MASKED = -1e30 / SCALE
MESH = pl.DeviceIdType.MESH
F32, BF16 = jnp.float32, jnp.bfloat16
NT = (((1,), (1,)), ((), ()))
NN = (((1,), (0,)), ((), ()))


def dot(a, b, dims=NN):
    return lax.dot_general(a, b, dims, preferred_element_type=F32)


def kernel(
    len_s, own_s, grp_s,
    q_h, k_h, v_h, pk_h, pv_h, w_h, cot_h,
    bo_h, gq_h, gk_h, gv_h, gpk_h, gpv_h,
    w_s, cot_s, ga_acc, ga_t, q3, kall, vall, kt_s, vt_s, parts_k, parts_v, pick_k, pick_v,
    mask_s, pt_s, ds_s, delta_s, att_s, dk_acc, dv_acc, gq_s, gkv_s,
    g_k, g_v, rg_k, rg_v, qs_k, qs_v, rq_k, rq_v, u_k, u_v, fin_k, fin_v, out_k, out_v,
    pb, rb1, acc, rs1, rs2, bo_s, inv_s,
    loc, z1s, z1r, y2s, y2r, z3s, z3r, xs, xr, ps, pr,
    b3s, b3r, b2s, b2r, b1s, b1r, cs, cr, r1s, r1r, r2s, r2r,
):
    me = lax.axis_index("dp")
    t = lax.axis_index("tensor")
    y, z = me // Z, me % Z
    x, c = t // 2, t % 2
    right = lax.rem(x + 1, X)
    left = lax.rem(x + X - 1, X)
    opp = lax.rem(x + 2, X)

    def at_z(d):
        return (y * Z + lax.rem(z + d, Z), t)

    def at_y(d):
        return (lax.rem(y + d, Y) * Z + z, t)

    to_right = (me, right * 2 + c)
    to_left = (me, left * 2 + c)
    partner = (me, x * 2 + 1 - c)
    sent = []

    def send(src, dst, ss, rs, dev):
        cp = pltpu.make_async_remote_copy(
            src_ref=src, dst_ref=dst, send_sem=ss, recv_sem=rs, device_id=dev, device_id_type=MESH
        )
        cp.start()
        sent.append(cp)
        return cp

    lane = pl.ds(pl.multiple_of(c * BLK, 128), BLK)
    loads = [
        pltpu.make_async_copy(cot_h, cot_s.at[x, :, lane], loc.at[0]),
        pltpu.make_async_copy(k_h, kall.at[pl.ds(4, 2)], loc.at[1]),
        pltpu.make_async_copy(v_h, vall.at[pl.ds(4, 2)], loc.at[2]),
        pltpu.make_async_copy(pk_h.at[z], parts_k.at[me], loc.at[3]),
        pltpu.make_async_copy(pv_h.at[z], parts_v.at[me], loc.at[4]),
        pltpu.make_async_copy(w_h, w_s, loc.at[5]),
    ]
    for h in range(HEADS):
        loads.append(
            pltpu.make_async_copy(q_h.at[:, pl.ds(h * HEAD, HEAD)], q3.at[h], loc.at[6 + h])
        )
    for cp in loads:
        cp.start()

    barrier = pltpu.get_barrier_semaphore()
    peers = [at_z(d) for d in range(1, Z)] + [at_y(d) for d in range(1, Y)]
    peers += [to_right, to_left, partner]
    for dev in peers:
        pl.semaphore_signal(barrier, inc=1, device_id=dev, device_id_type=MESH)
    pl.semaphore_wait(barrier, len(peers))

    z1 = []
    for kv, (src, dst) in enumerate(((pk_h, parts_k), (pv_h, parts_v))):
        z1.append(
            [
                send(src.at[lax.rem(z + d, Z)], dst.at[me], z1s.at[kv, d], z1r.at[kv, d], at_z(d))
                for d in range(1, Z)
            ]
        )
    lo, hi = pl.ds(0, 128), pl.ds(128, 128)
    own_cot = cot_s.at[x]
    ra = send(cot_h.at[lo], own_cot.at[lo, lane], xs.at[0], xr.at[0], to_right)
    lb = send(cot_h.at[hi], own_cot.at[hi, lane], xs.at[1], xr.at[1], to_left)
    rb = send(cot_h.at[hi], own_cot.at[hi, lane], xs.at[2], xr.at[2], to_right)
    la = send(cot_h.at[lo], own_cot.at[lo, lane], xs.at[3], xr.at[3], to_left)
    p_own = send(cot_h, own_cot.at[:, lane], ps.at[0], pr.at[0], partner)

    def find(s, _):
        def scan(j, found):
            return jnp.where(own_s[j] == s, j, found)

        inv_s[s] = lax.fori_loop(0, Y * Z, scan, jnp.int32(0), unroll=True)
        return 0

    lax.fori_loop(0, Y * Z, find, 0)

    key_at = lax.broadcasted_iota(jnp.int32, (ROWS, ROWS), 0)
    query_at = lax.broadcasted_iota(jnp.int32, (ROWS, ROWS), 1)
    end0 = len_s[0, 0]
    end1 = end0 + len_s[0, 1]
    end2 = end1 + len_s[0, 2]

    def segment(at):
        return (
            (at >= end0).astype(jnp.int32)
            + (at >= end1).astype(jnp.int32)
            + (at >= end2).astype(jnp.int32)
        )

    seen = (segment(key_at) == segment(query_at)) & (key_at <= query_at)
    mask_s[...] = seen.astype(jnp.int32)
    dk_acc[...] = jnp.zeros_like(dk_acc)
    dv_acc[...] = jnp.zeros_like(dv_acc)

    def forward(block, rows, i, s):
        ref = cot_s.at[block, rows, lane]
        return send(ref, ref, ps.at[s], pr.at[s], partner)

    ra.wait_recv()
    ref = cot_s.at[left, lo, lane]
    fr = send(ref, ref, xs.at[4], xr.at[4], to_right)
    p_la = forward(left, lo, 0, 1)
    lb.wait_recv()
    ref = cot_s.at[right, hi, lane]
    fl = send(ref, ref, xs.at[5], xr.at[5], to_left)
    p_rb = forward(right, hi, 0, 2)

    y2 = []
    for kv, ref in enumerate((parts_k, parts_v)):
        loads[3 + kv].wait()
        for cp in z1[kv]:
            cp.wait_recv()
        rows = ref.at[pl.ds(y * Z, Z)]
        y2.append([send(rows, rows, y2s.at[kv, d], y2r.at[kv, d], at_y(d)) for d in range(1, Y)])

    def grad_att(block, first):
        cols = pl.ds(pl.multiple_of(block * PAIR, 128), PAIR)

        def step(i, _):
            rows = pl.ds(pl.multiple_of(i * 512, 512), 512)
            part = dot(w_s[rows, cols], cot_s[block], NT)
            ga_acc[rows, :] = part if first else ga_acc[rows, :] + part
            return 0

        lax.fori_loop(0, 2, step, 0)

    loads[0].wait()
    loads[5].wait()
    p_own.wait_recv()
    grad_att(x, True)

    rb.wait_recv()
    p_lb = forward(left, hi, 0, 3)
    la.wait_recv()
    p_ra = forward(right, lo, 0, 4)

    z3 = []
    for kv, (ref, pick, full) in enumerate(((parts_k, pick_k, kall), (parts_v, pick_v, vall))):
        for cp in y2[kv]:
            cp.wait_recv()

        def choose(dest, _, ref=ref, pick=pick):
            first = grp_s[y * Z + dest] * 4
            for p in range(4):
                pick[dest, p] = ref[inv_s[first + p]]
            return 0

        lax.fori_loop(0, Z, choose, 0)
        copies = []
        for d in range(1, Z):
            dest = lax.rem(z + d, Z)
            copies.append(
                send(
                    pick.at[dest], full.at[pl.ds(0, 4), z], z3s.at[kv, d], z3r.at[kv, d], at_z(d)
                )
            )
        for p in range(4):
            full[p, z] = pick[z, p]
        z3.append(copies)

    p_la.wait_recv()
    p_lb.wait_recv()
    grad_att(left, False)
    p_rb.wait_recv()
    p_ra.wait_recv()
    grad_att(right, False)
    fr.wait_recv()
    p_oa = forward(opp, lo, 0, 5)
    fl.wait_recv()
    p_ob = forward(opp, hi, 0, 6)
    p_oa.wait_recv()
    p_ob.wait_recv()
    grad_att(opp, False)
    ga_t[...] = ga_acc[...].astype(BF16).reshape(HEADS, HEAD, ROWS)

    for cp in loads[1:3] + loads[6:]:
        cp.wait()
    for copies in z3:
        for cp in copies:
            cp.wait_recv()
    kt_s[...] = kall[...].reshape(KEYS, HEAD).T
    vt_s[...] = vall[...].reshape(KEYS, HEAD).T

    def forward_head(h, _):
        keys = kall[...].reshape(KEYS, HEAD)
        st = dot(keys, q3[h], NT)
        s0 = st[:PROMPT]
        s1 = jnp.where(mask_s[...] != 0, st[PROMPT:], MASKED)
        top = jnp.maximum(jnp.max(s0, 0, keepdims=True), jnp.max(s1, 0, keepdims=True))
        e0 = jnp.exp2((s0 - top) * EXP_SCALE)
        e1 = jnp.exp2((s1 - top) * EXP_SCALE)
        total = jnp.sum(e0, 0, keepdims=True) + jnp.sum(e1, 0, keepdims=True)
        inverse = 1.0 / total
        pt_s[h, :PROMPT] = (e0 * inverse).astype(BF16)
        pt_s[h, PROMPT:] = (e1 * inverse).astype(BF16)
        probs = pt_s[h]
        grad = ga_t[h]
        out_t = dot(vt_s[...], probs)
        low = out_t.astype(BF16).astype(F32)
        delta_s[h] = jnp.sum(low * grad.astype(F32), 0, keepdims=True)
        att_s[:, pl.ds(pl.multiple_of(h * HEAD, HEAD), HEAD)] = out_t.T.astype(BF16)
        dv_acc[...] += dot(probs, grad, NT)
        return 0

    lax.fori_loop(0, HEADS, forward_head, 0)

    def reduce_start(kv, grad, g_ref, rg):
        g_ref[...] = grad[:PROMPT].astype(BF16).reshape(4, Z, 16, HEAD)
        rg[z] = g_ref[:, z]
        return [
            send(
                g_ref.at[:, lax.rem(z + d, Z)], rg.at[z], b3s.at[kv, d], b3r.at[kv, d], at_z(d)
            )
            for d in range(1, Z)
        ]

    b3 = [None, None]
    b2 = [None, None]
    b1 = [None, None]
    b3[1] = reduce_start(1, dv_acc[...], g_v, rg_v)
    gkv_s[1] = dv_acc[PROMPT:].astype(BF16)
    stores = [pltpu.make_async_copy(gkv_s.at[1], gv_h, loc.at[14])]
    stores[-1].start()

    def backward_head(h, _):
        values = vall[...].reshape(KEYS, HEAD)
        grad_p = dot(values, ga_t[h])
        low = (pt_s[h].astype(F32) * (grad_p - delta_s[h])).astype(BF16)
        ds_s[h] = low
        dk_acc[...] += dot(low, q3[h])
        return 0

    lax.fori_loop(0, HEADS, backward_head, 0)
    grad_k = dk_acc[...] * SCALE
    b3[0] = reduce_start(0, grad_k, g_k, rg_k)
    gkv_s[0] = grad_k[PROMPT:].astype(BF16)
    stores.append(pltpu.make_async_copy(gkv_s.at[0], gk_h, loc.at[15]))
    stores[-1].start()

    def query_head(h, _):
        dq = dot(kt_s[...], ds_s[h])
        gq_s[:, pl.ds(pl.multiple_of(h * HEAD, HEAD), HEAD)] = (dq.T * SCALE).astype(BF16)
        return 0

    lax.fori_loop(0, HEADS, query_head, 0)
    stores.append(pltpu.make_async_copy(gq_s, gq_h, loc.at[16]))
    stores[-1].start()

    def reduce_z(kv, rg, qs, rq):
        for cp in b3[kv]:
            cp.wait_recv()

        def slot(j, _):
            s = own_s[j]
            group, piece = s // 4, s % 4
            total = jnp.zeros((16, HEAD), F32)
            for source in range(Z):
                hit = jnp.full((16, HEAD), grp_s[y * Z + source], jnp.int32) == group
                total += jnp.where(hit, rg[source, piece].astype(F32), 0.0)
            qs[j] = total.astype(BF16)
            return 0

        lax.fori_loop(0, Y * Z, slot, 0)
        rq[y] = qs[pl.ds(y * Z, Z)]
        b2[kv] = [
            send(
                qs.at[pl.ds(lax.rem(y + d, Y) * Z, Z)],
                rq.at[y],
                b2s.at[kv, d],
                b2r.at[kv, d],
                at_y(d),
            )
            for d in range(1, Y)
        ]

    def reduce_y(kv, rq, u, fin):
        for cp in b2[kv]:
            cp.wait_recv()
        total = rq[0].astype(F32)
        for source in range(1, Y):
            total += rq[source].astype(F32)
        u[...] = total.astype(BF16)
        fin[z] = u[z]
        b1[kv] = [
            send(u.at[lax.rem(z + d, Z)], fin.at[z], b1s.at[kv, d], b1r.at[kv, d], at_z(d))
            for d in range(1, Z)
        ]

    def reduce_end(kv, fin, out, dst):
        for cp in b1[kv]:
            cp.wait_recv()
        out[...] = fin[...].astype(F32)
        stores.append(pltpu.make_async_copy(out, dst, loc.at[17 + kv]))
        stores[-1].start()

    core = [None] * CH
    one = [None] * CH
    two = [None] * CH

    def product(n):
        def step(i, _):
            cols = pl.ds(pl.multiple_of(n * CW + i * SUB, SUB), SUB)
            part = dot(att_s[...], w_s[:, cols]).astype(BF16)
            pb[n, :, :, :, pl.ds(pl.multiple_of(i * SUB, SUB), SUB)] = part.reshape(X, 2, 32, SUB)
            return 0

        lax.fori_loop(0, CW // SUB, step, 0)
        core[n] = send(pb.at[n, :, 1 - c], rb1.at[n], cs.at[n], cr.at[n], partner)

    def ring_one(n):
        core[n].wait_recv()
        for d in range(X):
            b = lax.rem(x + d, X)
            acc[n, d] = (pb[n, b, c].astype(F32) + rb1[n, b].astype(F32)).astype(BF16)
        one[n] = (
            send(acc.at[n, 2, pl.ds(0, 16)], rs1.at[n, 0], r1s.at[n, 0], r1r.at[n, 0], to_right),
            send(acc.at[n, 2, pl.ds(16, 16)], rs1.at[n, 1], r1s.at[n, 1], r1r.at[n, 1], to_left),
        )

    def ring_two(n):
        one[n][0].wait_recv()
        acc[n, 1, :16] = (acc[n, 1, :16].astype(F32) + rs1[n, 0].astype(F32)).astype(BF16)
        first = send(acc.at[n, 1], rs2.at[n, 0], r2s.at[n, 0], r2r.at[n, 0], to_right)
        one[n][1].wait_recv()
        acc[n, 3, 16:] = (acc[n, 3, 16:].astype(F32) + rs1[n, 1].astype(F32)).astype(BF16)
        two[n] = (
            first,
            send(acc.at[n, 3], rs2.at[n, 1], r2s.at[n, 1], r2r.at[n, 1], to_left),
        )

    def ring_end(n):
        two[n][0].wait_recv()
        two[n][1].wait_recv()
        total = acc[n, 0].astype(F32) + rs2[n, 0].astype(F32) + rs2[n, 1].astype(F32)
        bo_s[:, n * CW : (n + 1) * CW] = total.astype(BF16)

    product(0)
    product(1)
    ring_one(0)
    reduce_z(1, rg_v, qs_v, rq_v)
    product(2)
    ring_one(1)
    product(3)
    ring_one(2)
    reduce_z(0, rg_k, qs_k, rq_k)
    ring_two(0)
    ring_one(3)
    ring_two(1)
    reduce_y(1, rq_v, u_v, fin_v)
    ring_two(2)
    ring_two(3)
    reduce_y(0, rq_k, u_k, fin_k)
    ring_end(0)
    ring_end(1)
    reduce_end(1, fin_v, out_v, gpv_h)
    ring_end(2)
    ring_end(3)
    stores.append(pltpu.make_async_copy(bo_s, bo_h, loc.at[19]))
    stores[-1].start()
    reduce_end(0, fin_k, out_k, gpk_h)
    for cp in sent:
        cp.wait_send()
    for cp in stores:
        cp.wait()


def local(
    queries, keys, values, prompt_keys, prompt_values,
    lengths, owner_slice, device_group, out_weight, cotangent,
):
    smem = pl.BlockSpec(memory_space=pltpu.SMEM)
    hbm = pl.BlockSpec(memory_space=pl.ANY)
    vm = pltpu.VMEM
    dma = pltpu.SemaphoreType.DMA
    tile = (16, HEAD)
    scratch = [
        vm((HEADS * HEAD, D), BF16),
        vm((X, ROWS, PAIR), BF16),
        vm((HEADS * HEAD, ROWS), F32),
        vm((HEADS, HEAD, ROWS), BF16),
        vm((HEADS, ROWS, HEAD), BF16),
        vm((6, Z) + tile, BF16),
        vm((6, Z) + tile, BF16),
        vm((HEAD, KEYS), BF16),
        vm((HEAD, KEYS), BF16),
        vm((Y * Z,) + tile, BF16),
        vm((Y * Z,) + tile, BF16),
        vm((Z, 4) + tile, BF16),
        vm((Z, 4) + tile, BF16),
        vm((ROWS, ROWS), jnp.int32),
        vm((HEADS, KEYS, ROWS), BF16),
        vm((HEADS, KEYS, ROWS), BF16),
        vm((HEADS, 1, ROWS), F32),
        vm((ROWS, HEADS * HEAD), BF16),
        vm((KEYS, HEAD), F32),
        vm((KEYS, HEAD), F32),
        vm((ROWS, HEADS * HEAD), BF16),
        vm((2, ROWS, HEAD), BF16),
        vm((4, Z) + tile, BF16),
        vm((4, Z) + tile, BF16),
        vm((Z, 4) + tile, BF16),
        vm((Z, 4) + tile, BF16),
        vm((Y * Z,) + tile, BF16),
        vm((Y * Z,) + tile, BF16),
        vm((Y, Z) + tile, BF16),
        vm((Y, Z) + tile, BF16),
        vm((Z,) + tile, BF16),
        vm((Z,) + tile, BF16),
        vm((Z,) + tile, BF16),
        vm((Z,) + tile, BF16),
        vm((Z,) + tile, F32),
        vm((Z,) + tile, F32),
        vm((CH, X, 2, 32, CW), BF16),
        vm((CH, X, 32, CW), BF16),
        vm((CH, X, 32, CW), BF16),
        vm((CH, 2, 16, CW), BF16),
        vm((CH, 2, 32, CW), BF16),
        vm((32, D), BF16),
        pltpu.SMEM((Y * Z,), jnp.int32),
        dma((20,)),
        dma((2, Z)), dma((2, Z)),
        dma((2, Y)), dma((2, Y)),
        dma((2, Z)), dma((2, Z)),
        dma((6,)), dma((6,)),
        dma((7,)), dma((7,)),
        dma((2, Z)), dma((2, Z)),
        dma((2, Y)), dma((2, Y)),
        dma((2, Z)), dma((2, Z)),
        dma((CH,)), dma((CH,)),
        dma((CH, 2)), dma((CH, 2)),
        dma((CH, 2)), dma((CH, 2)),
    ]
    shape = jax.ShapeDtypeStruct
    outs = pl.pallas_call(
        kernel,
        out_shape=(
            shape((32, D), BF16),
            shape((ROWS, HEADS * HEAD), BF16),
            shape((ROWS, HEAD), BF16),
            shape((ROWS, HEAD), BF16),
            shape((Z,) + tile, F32),
            shape((Z,) + tile, F32),
        ),
        in_specs=[smem] * 3 + [hbm] * 7,
        out_specs=[hbm] * 6,
        scratch_shapes=scratch,
        compiler_params=pltpu.CompilerParams(
            collective_id=0, has_side_effects=True, vmem_limit_bytes=58 * 1024 * 1024
        ),
        name="attention_block",
    )(
        lengths,
        owner_slice,
        device_group,
        queries,
        keys.reshape(2, Z, 16, HEAD),
        values.reshape(2, Z, 16, HEAD),
        prompt_keys.reshape(Z, 16, HEAD),
        prompt_values.reshape(Z, 16, HEAD),
        out_weight,
        cotangent,
    )
    return outs[:4] + (outs[4].reshape(128, HEAD), outs[5].reshape(128, HEAD))


def solution(mesh):
    placed = (
        P("dp", "tensor"),
        P("dp", "tensor"),
        P("dp", "tensor"),
        P("dp", "tensor"),
        P("dp", "tensor"),
        P("dp", None),
        P(),
        P(),
        P("tensor", None),
        P("dp", "tensor"),
    )
    return jax.shard_map(
        local,
        mesh=mesh,
        in_specs=placed,
        out_specs=(
            P(("dp", "tensor"), None),
            P("dp", "tensor"),
            P("dp", "tensor"),
            P("dp", "tensor"),
            P("dp", "tensor"),
            P("dp", "tensor"),
        ),
        check_vma=False,
    )
```

```python
import functools

import jax
import jax.numpy as jnp
from jax import lax
from jax.experimental import pallas as pl
from jax.experimental.pallas import tpu as pltpu
from jax.sharding import PartitionSpec as P

Y, Z, X = 4, 8, 4
HEAD = 128
HEADS = 8
ROWS = 256
PROMPT = 512
KEYS = PROMPT + ROWS
D = 5120
BLK = D // 8
PAIR = 2 * BLK
CH = 4
CW = D // CH
SCALE = HEAD**-0.5
EXP_SCALE = SCALE * 1.4426950408889634
MASKED = -1e30 / SCALE
MESH = pl.DeviceIdType.MESH
F32, BF16 = jnp.float32, jnp.bfloat16
NT = (((1,), (1,)), ((), ()))
NN = (((1,), (0,)), ((), ()))


def dot(a, b, dims=NN):
    return lax.dot_general(a, b, dims, preferred_element_type=F32)


def kernel(
    len_s, own_s, grp_s,
    q_h, k_h, v_h, pk_h, pv_h, w_h, cot_h,
    bo_h, gq_h, gk_h, gv_h, gpk_h, gpv_h,
    w_s, cot_s, ga_acc, ga_t, q3, kall, vall, kt_s, vt_s, parts_k, parts_v, pick_k, pick_v,
    mask_s, pt_s, ds_s, ga_n, inverse_s, delta_s, att_s, gq_s, gkv_s,
    g_k, g_v, rg_k, rg_v, qs_k, qs_v, rq_k, rq_v, u_k, u_v, fin_k, fin_v, out_k, out_v,
    pb, rb1, acc, rs1, rs2, bo_s, inv_s,
    loc, z1s, z1r, y2s, y2r, z3s, z3r, xs, xr, ps, pr,
    b3s, b3r, b2s, b2r, b1s, b1r, cs, cr, r1s, r1r, r2s, r2r,
):
    me = lax.axis_index("dp")
    t = lax.axis_index("tensor")
    y, z = me // Z, me % Z
    x, c = t // 2, t % 2
    right = lax.rem(x + 1, X)
    left = lax.rem(x + X - 1, X)
    opp = lax.rem(x + 2, X)

    def at_z(d):
        return (y * Z + lax.rem(z + d, Z), t)

    def at_y(d):
        return (lax.rem(y + d, Y) * Z + z, t)

    to_right = (me, right * 2 + c)
    to_left = (me, left * 2 + c)
    partner = (me, x * 2 + 1 - c)
    sent = []

    def send(src, dst, ss, rs, dev):
        cp = pltpu.make_async_remote_copy(
            src_ref=src, dst_ref=dst, send_sem=ss, recv_sem=rs, device_id=dev, device_id_type=MESH
        )
        cp.start()
        sent.append(cp)
        return cp

    lane = pl.ds(pl.multiple_of(c * BLK, 128), BLK)
    loads = [
        pltpu.make_async_copy(pk_h.at[z], parts_k.at[me], loc.at[3]),
        pltpu.make_async_copy(pv_h.at[z], parts_v.at[me], loc.at[4]),
        pltpu.make_async_copy(cot_h, cot_s.at[x, :, lane], loc.at[0]),
        pltpu.make_async_copy(k_h, kall.at[pl.ds(4, 2)], loc.at[1]),
        pltpu.make_async_copy(v_h, vall.at[pl.ds(4, 2)], loc.at[2]),
        pltpu.make_async_copy(w_h, w_s, loc.at[5]),
    ]
    for h in range(HEADS):
        loads.append(
            pltpu.make_async_copy(q_h.at[:, pl.ds(h * HEAD, HEAD)], q3.at[h], loc.at[6 + h])
        )
    for cp in loads:
        cp.start()

    barrier = pltpu.get_barrier_semaphore()
    peers = [at_z(d) for d in range(1, Z)] + [at_y(d) for d in range(1, Y)]
    peers += [to_right, to_left, partner]
    for dev in peers:
        pl.semaphore_signal(barrier, inc=1, device_id=dev, device_id_type=MESH)
    pl.semaphore_wait(barrier, len(peers))

    z1 = []
    for kv, (src, dst) in enumerate(((pk_h, parts_k), (pv_h, parts_v))):
        z1.append(
            [
                send(src.at[lax.rem(z + d, Z)], dst.at[me], z1s.at[kv, d], z1r.at[kv, d], at_z(d))
                for d in range(1, Z)
            ]
        )
    lo, hi = pl.ds(0, 128), pl.ds(128, 128)
    own_cot = cot_s.at[x]
    ra = send(cot_h.at[lo], own_cot.at[lo, lane], xs.at[0], xr.at[0], to_right)
    lb = send(cot_h.at[hi], own_cot.at[hi, lane], xs.at[1], xr.at[1], to_left)
    rb = send(cot_h.at[hi], own_cot.at[hi, lane], xs.at[2], xr.at[2], to_right)
    la = send(cot_h.at[lo], own_cot.at[lo, lane], xs.at[3], xr.at[3], to_left)
    p_own = send(cot_h, own_cot.at[:, lane], ps.at[0], pr.at[0], partner)

    def find(s, _):
        def scan(j, found):
            return jnp.where(own_s[j] == s, j, found)

        inv_s[s] = lax.fori_loop(0, Y * Z, scan, jnp.int32(0), unroll=True)
        return 0

    lax.fori_loop(0, Y * Z, find, 0)

    key_at = lax.broadcasted_iota(jnp.int32, (ROWS, ROWS), 0)
    query_at = lax.broadcasted_iota(jnp.int32, (ROWS, ROWS), 1)
    end0 = len_s[0, 0]
    end1 = end0 + len_s[0, 1]
    end2 = end1 + len_s[0, 2]

    def segment(at):
        return (
            (at >= end0).astype(jnp.int32)
            + (at >= end1).astype(jnp.int32)
            + (at >= end2).astype(jnp.int32)
        )

    seen = (segment(key_at) == segment(query_at)) & (key_at <= query_at)
    mask_s[...] = seen.astype(jnp.int32)

    def forward(block, rows, s):
        ref = cot_s.at[block, rows, lane]
        return send(ref, ref, ps.at[s], pr.at[s], partner)

    def grad_att(block, first=False, last=False):
        cols = pl.ds(pl.multiple_of(block * PAIR, 128), PAIR)
        part = dot(w_s[:, cols], cot_s[block], NT)
        if first:
            ga_acc[...] = part
        elif last:
            ga_t[...] = (ga_acc[...] + part).astype(BF16).reshape(HEADS, HEAD, ROWS)
        else:
            ga_acc[...] += part

    y2 = []
    for kv, ref in enumerate((parts_k, parts_v)):
        loads[kv].wait()
        for cp in z1[kv]:
            cp.wait_recv()
        rows = ref.at[pl.ds(y * Z, Z)]
        y2.append([send(rows, rows, y2s.at[kv, d], y2r.at[kv, d], at_y(d)) for d in range(1, Y)])

    ra.wait_recv()
    ref = cot_s.at[left, lo, lane]
    fr = send(ref, ref, xs.at[4], xr.at[4], to_right)
    lb.wait_recv()
    ref = cot_s.at[right, hi, lane]
    fl = send(ref, ref, xs.at[5], xr.at[5], to_left)
    p_la = forward(left, lo, 1)
    p_rb = forward(right, hi, 2)

    loads[2].wait()
    loads[5].wait()
    p_own.wait_recv()
    grad_att(x, first=True)

    z3 = []
    for kv, (ref, pick, full) in enumerate(((parts_k, pick_k, kall), (parts_v, pick_v, vall))):
        for cp in y2[kv]:
            cp.wait_recv()

        def choose(dest, _, ref=ref, pick=pick):
            first = grp_s[y * Z + dest] * 4
            for p in range(4):
                pick[dest, p] = ref[inv_s[first + p]]
            return 0

        lax.fori_loop(0, Z, choose, 0, unroll=True)
        copies = []
        for d in range(1, Z):
            dest = lax.rem(z + d, Z)
            copies.append(
                send(
                    pick.at[dest], full.at[pl.ds(0, 4), z], z3s.at[kv, d], z3r.at[kv, d], at_z(d)
                )
            )
        for p in range(4):
            full[p, z] = pick[z, p]
        z3.append(copies)

    rb.wait_recv()
    p_lb = forward(left, hi, 3)
    la.wait_recv()
    p_ra = forward(right, lo, 4)
    p_la.wait_recv()
    p_lb.wait_recv()
    grad_att(left)
    fr.wait_recv()
    p_oa = forward(opp, lo, 5)
    fl.wait_recv()
    p_ob = forward(opp, hi, 6)
    p_rb.wait_recv()
    p_ra.wait_recv()
    grad_att(right)

    for cp in loads[3:5] + loads[6:]:
        cp.wait()
    for cp in z3[0]:
        cp.wait_recv()
    kt_s[...] = kall[...].reshape(KEYS, HEAD).T

    def queries_of(h):
        return pl.ds(pl.multiple_of(h * ROWS, ROWS), ROWS)

    def features_of(h):
        return pl.ds(pl.multiple_of(h * HEAD, HEAD), HEAD)

    def score_head(h, _):
        st = dot(kall[...].reshape(KEYS, HEAD), q3[h], NT)
        s0 = st[:PROMPT]
        s1 = jnp.where(mask_s[...] != 0, st[PROMPT:], MASKED)
        top = jnp.maximum(jnp.max(s0, 0, keepdims=True), jnp.max(s1, 0, keepdims=True))
        e0 = jnp.exp2((s0 - top) * EXP_SCALE)
        e1 = jnp.exp2((s1 - top) * EXP_SCALE)
        total = jnp.sum(e0, 0, keepdims=True) + jnp.sum(e1, 0, keepdims=True)
        inverse_s[h] = 1.0 / total
        pt_s[:PROMPT, queries_of(h)] = e0.astype(BF16)
        pt_s[PROMPT:, queries_of(h)] = e1.astype(BF16)
        return 0

    lax.fori_loop(0, HEADS, score_head, 0, unroll=True)

    p_oa.wait_recv()
    p_ob.wait_recv()
    grad_att(opp, last=True)

    for cp in z3[1]:
        cp.wait_recv()
    vt_s[...] = vall[...].reshape(KEYS, HEAD).T

    def value_head(h, _):
        inverse = inverse_s[h]
        out_t = dot(vt_s[...], pt_s[:, queries_of(h)]) * inverse
        low = out_t.astype(BF16).astype(F32)
        grad = ga_t[h].astype(F32)
        delta_s[h] = jnp.sum(low * grad, 0, keepdims=True) * inverse
        ga_n[:, queries_of(h)] = (grad * inverse).astype(BF16)
        att_s[:, features_of(h)] = out_t.T.astype(BF16)
        return 0

    lax.fori_loop(0, HEADS, value_head, 0, unroll=True)

    def reduce_start(kv, grad, g_ref, rg):
        g_ref[...] = grad[:PROMPT].astype(BF16).reshape(4, Z, 16, HEAD)
        rg[z] = g_ref[:, z]
        return [
            send(
                g_ref.at[:, lax.rem(z + d, Z)], rg.at[z], b3s.at[kv, d], b3r.at[kv, d], at_z(d)
            )
            for d in range(1, Z)
        ]

    b3 = [None, None]
    b2 = [None, None]
    b1 = [None, None]
    grad_v = dot(pt_s[...], ga_n[...], NT)
    b3[1] = reduce_start(1, grad_v, g_v, rg_v)
    gkv_s[1] = grad_v[PROMPT:].astype(BF16)
    stores = [pltpu.make_async_copy(gkv_s.at[1], gv_h, loc.at[14])]
    stores[-1].start()

    def backward_head(h, _):
        grad_p = dot(vall[...].reshape(KEYS, HEAD), ga_n[:, queries_of(h)])
        probs = pt_s[:, queries_of(h)].astype(F32)
        ds_s[:, queries_of(h)] = (probs * (grad_p - delta_s[h])).astype(BF16)
        return 0

    lax.fori_loop(0, HEADS, backward_head, 0, unroll=True)
    grad_k = dot(ds_s[...], q3[...].reshape(HEADS * ROWS, HEAD)) * SCALE
    b3[0] = reduce_start(0, grad_k, g_k, rg_k)
    gkv_s[0] = grad_k[PROMPT:].astype(BF16)
    stores.append(pltpu.make_async_copy(gkv_s.at[0], gk_h, loc.at[15]))
    stores[-1].start()

    def query_head(h, _):
        dq = dot(kt_s[...], ds_s[:, queries_of(h)])
        gq_s[:, features_of(h)] = (dq.T * SCALE).astype(BF16)
        return 0

    def reduce_z(kv, rg, qs, rq):
        for cp in b3[kv]:
            cp.wait_recv()

        def slot(j, _):
            s = own_s[j]
            group, piece = s // 4, s % 4
            total = jnp.zeros((16, HEAD), F32)
            for source in range(Z):
                hit = jnp.full((16, HEAD), grp_s[y * Z + source], jnp.int32) == group
                total += jnp.where(hit, rg[source, piece].astype(F32), 0.0)
            qs[j] = total.astype(BF16)
            return 0

        lax.fori_loop(0, Y * Z, slot, 0, unroll=4)
        rq[y] = qs[pl.ds(y * Z, Z)]
        b2[kv] = [
            send(
                qs.at[pl.ds(lax.rem(y + d, Y) * Z, Z)],
                rq.at[y],
                b2s.at[kv, d],
                b2r.at[kv, d],
                at_y(d),
            )
            for d in range(1, Y)
        ]

    def reduce_y(kv, rq, u, fin):
        for cp in b2[kv]:
            cp.wait_recv()
        total = rq[0].astype(F32)
        for source in range(1, Y):
            total += rq[source].astype(F32)
        u[...] = total.astype(BF16)
        fin[z] = u[z]
        b1[kv] = [
            send(u.at[lax.rem(z + d, Z)], fin.at[z], b1s.at[kv, d], b1r.at[kv, d], at_z(d))
            for d in range(1, Z)
        ]

    def reduce_end(kv, fin, out, dst):
        for cp in b1[kv]:
            cp.wait_recv()
        out[...] = fin[...].astype(F32)
        stores.append(pltpu.make_async_copy(out, dst, loc.at[17 + kv]))
        stores[-1].start()

    core = [None] * CH
    one = [None] * CH
    two = [None] * CH

    def product(n):
        part = dot(att_s[...], w_s[:, n * CW : (n + 1) * CW])
        pb[n] = part.astype(BF16).reshape(X, 2, 32, CW)
        core[n] = send(pb.at[n, :, 1 - c], rb1.at[n], cs.at[n], cr.at[n], partner)

    def ring_one(n):
        core[n].wait_recv()
        for d in range(X):
            b = lax.rem(x + d, X)
            acc[n, d] = (pb[n, b, c].astype(F32) + rb1[n, b].astype(F32)).astype(BF16)
        one[n] = (
            send(acc.at[n, 2, pl.ds(0, 16)], rs1.at[n, 0], r1s.at[n, 0], r1r.at[n, 0], to_right),
            send(acc.at[n, 2, pl.ds(16, 16)], rs1.at[n, 1], r1s.at[n, 1], r1r.at[n, 1], to_left),
        )

    def ring_two(n):
        one[n][0].wait_recv()
        acc[n, 1, :16] = (acc[n, 1, :16].astype(F32) + rs1[n, 0].astype(F32)).astype(BF16)
        first = send(acc.at[n, 1], rs2.at[n, 0], r2s.at[n, 0], r2r.at[n, 0], to_right)
        one[n][1].wait_recv()
        acc[n, 3, 16:] = (acc[n, 3, 16:].astype(F32) + rs1[n, 1].astype(F32)).astype(BF16)
        two[n] = (
            first,
            send(acc.at[n, 3], rs2.at[n, 1], r2s.at[n, 1], r2r.at[n, 1], to_left),
        )

    def ring_end(n):
        two[n][0].wait_recv()
        two[n][1].wait_recv()
        total = acc[n, 0].astype(F32) + rs2[n, 0].astype(F32) + rs2[n, 1].astype(F32)
        bo_s[:, n * CW : (n + 1) * CW] = total.astype(BF16)

    product(0)
    product(1)
    ring_one(0)
    product(2)
    ring_one(1)
    product(3)
    lax.fori_loop(0, HEADS, query_head, 0, unroll=True)
    stores.append(pltpu.make_async_copy(gq_s, gq_h, loc.at[16]))
    stores[-1].start()
    reduce_z(1, rg_v, qs_v, rq_v)
    ring_one(2)
    ring_one(3)
    ring_two(0)
    reduce_z(0, rg_k, qs_k, rq_k)
    ring_two(1)
    reduce_y(1, rq_v, u_v, fin_v)
    ring_two(2)
    ring_two(3)
    reduce_y(0, rq_k, u_k, fin_k)
    early = len(sent)
    for cp in sent[: early - 2 * Z]:
        cp.wait_send()
    ring_end(0)
    ring_end(1)
    reduce_end(1, fin_v, out_v, gpv_h)
    ring_end(2)
    ring_end(3)
    stores.append(pltpu.make_async_copy(bo_s, bo_h, loc.at[19]))
    stores[-1].start()
    reduce_end(0, fin_k, out_k, gpk_h)
    for cp in sent[early - 2 * Z :]:
        cp.wait_send()
    for cp in stores:
        cp.wait()


def place(*refs):
    n = len(refs) // 2
    sem = refs[-1]
    copies = [pltpu.make_async_copy(refs[i], refs[n + i], sem.at[i]) for i in range(n)]
    for cp in copies:
        cp.start()
    for cp in copies:
        cp.wait()


def local(
    queries, keys, values, prompt_keys, prompt_values,
    lengths, owner_slice, device_group, out_weight, cotangent,
):
    smem = pl.BlockSpec(memory_space=pltpu.SMEM)
    hbm = pl.BlockSpec(memory_space=pl.ANY)
    vm = pltpu.VMEM
    dma = pltpu.SemaphoreType.DMA
    tile = (16, HEAD)
    scratch = [
        vm((HEADS * HEAD, D), BF16),
        vm((X, ROWS, PAIR), BF16),
        vm((HEADS * HEAD, ROWS), F32),
        vm((HEADS, HEAD, ROWS), BF16),
        vm((HEADS, ROWS, HEAD), BF16),
        vm((6, Z) + tile, BF16),
        vm((6, Z) + tile, BF16),
        vm((HEAD, KEYS), BF16),
        vm((HEAD, KEYS), BF16),
        vm((Y * Z,) + tile, BF16),
        vm((Y * Z,) + tile, BF16),
        vm((Z, 4) + tile, BF16),
        vm((Z, 4) + tile, BF16),
        vm((ROWS, ROWS), jnp.int32),
        vm((KEYS, HEADS * ROWS), BF16),
        vm((KEYS, HEADS * ROWS), BF16),
        vm((HEAD, HEADS * ROWS), BF16),
        vm((HEADS, 1, ROWS), F32),
        vm((HEADS, 1, ROWS), F32),
        vm((ROWS, HEADS * HEAD), BF16),
        vm((ROWS, HEADS * HEAD), BF16),
        vm((2, ROWS, HEAD), BF16),
        vm((4, Z) + tile, BF16),
        vm((4, Z) + tile, BF16),
        vm((Z, 4) + tile, BF16),
        vm((Z, 4) + tile, BF16),
        vm((Y * Z,) + tile, BF16),
        vm((Y * Z,) + tile, BF16),
        vm((Y, Z) + tile, BF16),
        vm((Y, Z) + tile, BF16),
        vm((Z,) + tile, BF16),
        vm((Z,) + tile, BF16),
        vm((Z,) + tile, BF16),
        vm((Z,) + tile, BF16),
        vm((Z,) + tile, F32),
        vm((Z,) + tile, F32),
        vm((CH, X, 2, 32, CW), BF16),
        vm((CH, X, 32, CW), BF16),
        vm((CH, X, 32, CW), BF16),
        vm((CH, 2, 16, CW), BF16),
        vm((CH, 2, 32, CW), BF16),
        vm((32, D), BF16),
        pltpu.SMEM((Y * Z,), jnp.int32),
        dma((20,)),
        dma((2, Z)), dma((2, Z)),
        dma((2, Y)), dma((2, Y)),
        dma((2, Z)), dma((2, Z)),
        dma((6,)), dma((6,)),
        dma((7,)), dma((7,)),
        dma((2, Z)), dma((2, Z)),
        dma((2, Y)), dma((2, Y)),
        dma((2, Z)), dma((2, Z)),
        dma((CH,)), dma((CH,)),
        dma((CH, 2)), dma((CH, 2)),
        dma((CH, 2)), dma((CH, 2)),
    ]
    shape = jax.ShapeDtypeStruct
    outs = pl.pallas_call(
        kernel,
        out_shape=(
            shape((32, D), BF16),
            shape((ROWS, HEADS * HEAD), BF16),
            shape((ROWS, HEAD), BF16),
            shape((ROWS, HEAD), BF16),
            shape((Z,) + tile, F32),
            shape((Z,) + tile, F32),
        ),
        in_specs=[smem] * 3 + [hbm] * 7,
        out_specs=[hbm] * 6,
        scratch_shapes=scratch,
        compiler_params=pltpu.CompilerParams(
            collective_id=0, has_side_effects=True, vmem_limit_bytes=58 * 1024 * 1024
        ),
        name="attention_block",
    )(
        lengths,
        owner_slice,
        device_group,
        queries,
        keys.reshape(2, Z, 16, HEAD),
        values.reshape(2, Z, 16, HEAD),
        prompt_keys.reshape(Z, 16, HEAD),
        prompt_values.reshape(Z, 16, HEAD),
        out_weight,
        cotangent,
    )
    outs = pl.pallas_call(
        place,
        out_shape=tuple(shape(o.shape, o.dtype) for o in outs),
        in_specs=[hbm] * 6,
        out_specs=[hbm] * 6,
        scratch_shapes=[dma((6,))],
        name="place",
    )(*outs)
    return outs[:4] + (outs[4].reshape(128, HEAD), outs[5].reshape(128, HEAD))


def solution(mesh):
    placed = (
        P("dp", "tensor"),
        P("dp", "tensor"),
        P("dp", "tensor"),
        P("dp", "tensor"),
        P("dp", "tensor"),
        P("dp", None),
        P(),
        P(),
        P("tensor", None),
        P("dp", "tensor"),
    )
    return jax.shard_map(
        local,
        mesh=mesh,
        in_specs=placed,
        out_specs=(
            P(("dp", "tensor"), None),
            P("dp", "tensor"),
            P("dp", "tensor"),
            P("dp", "tensor"),
            P("dp", "tensor"),
            P("dp", "tensor"),
        ),
        check_vma=False,
    )
```

```python
import functools

import jax
import jax.numpy as jnp
from jax import lax
from jax.experimental import pallas as pl
from jax.experimental.pallas import tpu as pltpu
from jax.sharding import PartitionSpec as P

Y, Z, X = 4, 8, 4
HEAD = 128
HEADS = 8
ROWS = 256
PROMPT = 512
KEYS = PROMPT + ROWS
D = 5120
BLK = D // 8
PAIR = 2 * BLK
CH = 4
CW = D // CH
SCALE = HEAD**-0.5
EXP_SCALE = SCALE * 1.4426950408889634
MASKED = -1e30 / SCALE
MESH = pl.DeviceIdType.MESH
F32, BF16 = jnp.float32, jnp.bfloat16
NT = (((1,), (1,)), ((), ()))
NN = (((1,), (0,)), ((), ()))


def dot(a, b, dims=NN):
    return lax.dot_general(a, b, dims, preferred_element_type=F32)


def kernel(
    len_s, own_s, grp_s,
    q_h, k_h, v_h, pk_h, pv_h, w_h, cot_h,
    bo_h, gq_h, gk_h, gv_h, gpk_h, gpv_h,
    w_s, cot_s, ga_acc, ga_t, q3, kall, vall, kt_s, vt_s, parts_k, parts_v, pick_k, pick_v,
    mask_s, pt_s, ds_s, ga_n, inverse_s, delta_s, att_s, gq_s, gkv_s,
    g_k, g_v, rg_k, rg_v, qs_k, qs_v, rq_k, rq_v, u_k, u_v, fin_k, fin_v, out_k, out_v,
    pb, rb1, acc, rs1, rs2, bo_s, inv_s,
    loc, z1s, z1r, y2s, y2r, z3s, z3r, xs, xr, ps, pr,
    b3s, b3r, b2s, b2r, b1s, b1r, cs, cr, r1s, r1r, r2s, r2r,
):
    me = lax.axis_index("dp")
    t = lax.axis_index("tensor")
    y, z = me // Z, me % Z
    x, c = t // 2, t % 2
    right = lax.rem(x + 1, X)
    left = lax.rem(x + X - 1, X)
    opp = lax.rem(x + 2, X)

    def at_z(d):
        return (y * Z + lax.rem(z + d, Z), t)

    def at_y(d):
        return (lax.rem(y + d, Y) * Z + z, t)

    to_right = (me, right * 2 + c)
    to_left = (me, left * 2 + c)
    partner = (me, x * 2 + 1 - c)
    sent = []

    def send(src, dst, ss, rs, dev):
        cp = pltpu.make_async_remote_copy(
            src_ref=src, dst_ref=dst, send_sem=ss, recv_sem=rs, device_id=dev, device_id_type=MESH
        )
        cp.start()
        sent.append(cp)
        return cp

    lane = pl.ds(pl.multiple_of(c * BLK, 128), BLK)
    loads = [
        pltpu.make_async_copy(pk_h.at[z], parts_k.at[me], loc.at[3]),
        pltpu.make_async_copy(pv_h.at[z], parts_v.at[me], loc.at[4]),
        pltpu.make_async_copy(cot_h, cot_s.at[x, :, lane], loc.at[0]),
        pltpu.make_async_copy(k_h, kall.at[pl.ds(4, 2)], loc.at[1]),
        pltpu.make_async_copy(v_h, vall.at[pl.ds(4, 2)], loc.at[2]),
        pltpu.make_async_copy(w_h, w_s, loc.at[5]),
    ]
    for h in range(HEADS):
        loads.append(
            pltpu.make_async_copy(q_h.at[:, pl.ds(h * HEAD, HEAD)], q3.at[h], loc.at[6 + h])
        )
    for cp in loads:
        cp.start()

    barrier = pltpu.get_barrier_semaphore()
    peers = [at_z(d) for d in range(1, Z)] + [at_y(d) for d in range(1, Y)]
    peers += [to_right, to_left, partner]
    for dev in peers:
        pl.semaphore_signal(barrier, inc=1, device_id=dev, device_id_type=MESH)
    pl.semaphore_wait(barrier, len(peers))

    z1 = []
    for kv, (src, dst) in enumerate(((pk_h, parts_k), (pv_h, parts_v))):
        z1.append(
            [
                send(src.at[lax.rem(z + d, Z)], dst.at[me], z1s.at[kv, d], z1r.at[kv, d], at_z(d))
                for d in range(1, Z)
            ]
        )
    lo, hi = pl.ds(0, 128), pl.ds(128, 128)
    own_cot = cot_s.at[x]
    ra = send(cot_h.at[lo], own_cot.at[lo, lane], xs.at[0], xr.at[0], to_right)
    lb = send(cot_h.at[hi], own_cot.at[hi, lane], xs.at[1], xr.at[1], to_left)
    rb = send(cot_h.at[hi], own_cot.at[hi, lane], xs.at[2], xr.at[2], to_right)
    la = send(cot_h.at[lo], own_cot.at[lo, lane], xs.at[3], xr.at[3], to_left)
    p_own = send(cot_h, own_cot.at[:, lane], ps.at[0], pr.at[0], partner)

    def find(s, _):
        def scan(j, found):
            return jnp.where(own_s[j] == s, j, found)

        inv_s[s] = lax.fori_loop(0, Y * Z, scan, jnp.int32(0), unroll=True)
        return 0

    lax.fori_loop(0, Y * Z, find, 0)

    key_at = lax.broadcasted_iota(jnp.int32, (ROWS, ROWS), 0)
    query_at = lax.broadcasted_iota(jnp.int32, (ROWS, ROWS), 1)
    end0 = len_s[0, 0]
    end1 = end0 + len_s[0, 1]
    end2 = end1 + len_s[0, 2]

    def segment(at):
        return (
            (at >= end0).astype(jnp.int32)
            + (at >= end1).astype(jnp.int32)
            + (at >= end2).astype(jnp.int32)
        )

    seen = (segment(key_at) == segment(query_at)) & (key_at <= query_at)
    mask_s[...] = seen.astype(jnp.int32)

    def forward(block, rows, s):
        ref = cot_s.at[block, rows, lane]
        return send(ref, ref, ps.at[s], pr.at[s], partner)

    def grad_att(block, first=False, last=False):
        cols = pl.ds(pl.multiple_of(block * PAIR, 128), PAIR)
        part = dot(w_s[:, cols], cot_s[block], NT)
        if first:
            ga_acc[...] = part
        elif last:
            ga_t[...] = (ga_acc[...] + part).astype(BF16).reshape(HEADS, HEAD, ROWS)
        else:
            ga_acc[...] += part

    y2 = []
    for kv, ref in enumerate((parts_k, parts_v)):
        loads[kv].wait()
        for cp in z1[kv]:
            cp.wait_recv()
        rows = ref.at[pl.ds(y * Z, Z)]
        y2.append([send(rows, rows, y2s.at[kv, d], y2r.at[kv, d], at_y(d)) for d in range(1, Y)])

    ra.wait_recv()
    ref = cot_s.at[left, lo, lane]
    fr = send(ref, ref, xs.at[4], xr.at[4], to_right)
    lb.wait_recv()
    ref = cot_s.at[right, hi, lane]
    fl = send(ref, ref, xs.at[5], xr.at[5], to_left)
    p_la = forward(left, lo, 1)
    p_rb = forward(right, hi, 2)

    loads[2].wait()
    loads[5].wait()
    p_own.wait_recv()
    grad_att(x, first=True)

    z3 = []
    for kv, (ref, pick, full) in enumerate(((parts_k, pick_k, kall), (parts_v, pick_v, vall))):
        for cp in y2[kv]:
            cp.wait_recv()

        def choose(dest, _, ref=ref, pick=pick):
            first = grp_s[y * Z + dest] * 4
            for p in range(4):
                pick[dest, p] = ref[inv_s[first + p]]
            return 0

        lax.fori_loop(0, Z, choose, 0, unroll=True)
        copies = []
        for d in range(1, Z):
            dest = lax.rem(z + d, Z)
            copies.append(
                send(
                    pick.at[dest], full.at[pl.ds(0, 4), z], z3s.at[kv, d], z3r.at[kv, d], at_z(d)
                )
            )
        for p in range(4):
            full[p, z] = pick[z, p]
        z3.append(copies)

    rb.wait_recv()
    p_lb = forward(left, hi, 3)
    la.wait_recv()
    p_ra = forward(right, lo, 4)
    p_la.wait_recv()
    p_lb.wait_recv()
    grad_att(left)
    fr.wait_recv()
    p_oa = forward(opp, lo, 5)
    fl.wait_recv()
    p_ob = forward(opp, hi, 6)
    p_rb.wait_recv()
    p_ra.wait_recv()
    grad_att(right)

    for cp in loads[3:5] + loads[6:]:
        cp.wait()
    for cp in z3[0]:
        cp.wait_recv()
    kt_s[...] = kall[...].reshape(KEYS, HEAD).T

    def queries_of(h):
        return pl.ds(pl.multiple_of(h * ROWS, ROWS), ROWS)

    def features_of(h):
        return pl.ds(pl.multiple_of(h * HEAD, HEAD), HEAD)

    def score_head(h, _):
        st = dot(kall[...].reshape(KEYS, HEAD), q3[h], NT)
        s0 = st[:PROMPT]
        s1 = jnp.where(mask_s[...] != 0, st[PROMPT:], MASKED)
        top = jnp.maximum(jnp.max(s0, 0, keepdims=True), jnp.max(s1, 0, keepdims=True))
        e0 = jnp.exp2((s0 - top) * EXP_SCALE)
        e1 = jnp.exp2((s1 - top) * EXP_SCALE)
        total = jnp.sum(e0, 0, keepdims=True) + jnp.sum(e1, 0, keepdims=True)
        inverse_s[h] = 1.0 / total
        pt_s[:PROMPT, queries_of(h)] = e0.astype(BF16)
        pt_s[PROMPT:, queries_of(h)] = e1.astype(BF16)
        return 0

    lax.fori_loop(0, HEADS, score_head, 0, unroll=True)

    p_oa.wait_recv()
    p_ob.wait_recv()
    grad_att(opp, last=True)

    for cp in z3[1]:
        cp.wait_recv()
    vt_s[...] = vall[...].reshape(KEYS, HEAD).T

    def value_head(h, _):
        inverse = inverse_s[h]
        out_t = dot(vt_s[...], pt_s[:, queries_of(h)]) * inverse
        low = out_t.astype(BF16).astype(F32)
        grad = ga_t[h].astype(F32)
        delta_s[h] = jnp.sum(low * grad, 0, keepdims=True) * inverse
        ga_n[:, queries_of(h)] = (grad * inverse).astype(BF16)
        att_s[:, features_of(h)] = out_t.T.astype(BF16)
        return 0

    lax.fori_loop(0, HEADS, value_head, 0, unroll=True)

    def reduce_start(kv, grad, g_ref, rg):
        g_ref[...] = grad[:PROMPT].astype(BF16).reshape(4, Z, 16, HEAD)
        rg[z] = g_ref[:, z]
        return [
            send(
                g_ref.at[:, lax.rem(z + d, Z)], rg.at[z], b3s.at[kv, d], b3r.at[kv, d], at_z(d)
            )
            for d in range(1, Z)
        ]

    b3 = [None, None]
    b2 = [None, None]
    b1 = [None, None]
    grad_v = dot(pt_s[...], ga_n[...], NT)
    b3[1] = reduce_start(1, grad_v, g_v, rg_v)
    gkv_s[1] = grad_v[PROMPT:].astype(BF16)
    stores = [pltpu.make_async_copy(gkv_s.at[1], gv_h, loc.at[14])]
    stores[-1].start()

    def backward_head(h, _):
        grad_p = dot(vall[...].reshape(KEYS, HEAD), ga_n[:, queries_of(h)])
        probs = pt_s[:, queries_of(h)].astype(F32)
        ds_s[:, queries_of(h)] = (probs * (grad_p - delta_s[h])).astype(BF16)
        return 0

    lax.fori_loop(0, HEADS, backward_head, 0, unroll=True)
    grad_k = dot(ds_s[...], q3[...].reshape(HEADS * ROWS, HEAD)) * SCALE
    b3[0] = reduce_start(0, grad_k, g_k, rg_k)
    gkv_s[0] = grad_k[PROMPT:].astype(BF16)
    stores.append(pltpu.make_async_copy(gkv_s.at[0], gk_h, loc.at[15]))
    stores[-1].start()

    def query_head(h, _):
        dq = dot(kt_s[...], ds_s[:, queries_of(h)])
        gq_s[:, features_of(h)] = (dq.T * SCALE).astype(BF16)
        return 0

    def reduce_z(kv, rg, qs, rq):
        for cp in b3[kv]:
            cp.wait_recv()

        def slot(j, _):
            s = own_s[j]
            group, piece = s // 4, s % 4
            total = jnp.zeros((16, HEAD), F32)
            for source in range(Z):
                hit = jnp.full((16, HEAD), grp_s[y * Z + source], jnp.int32) == group
                total += jnp.where(hit, rg[source, piece].astype(F32), 0.0)
            qs[j] = total.astype(BF16)
            return 0

        lax.fori_loop(0, Y * Z, slot, 0, unroll=4)
        rq[y] = qs[pl.ds(y * Z, Z)]
        b2[kv] = [
            send(
                qs.at[pl.ds(lax.rem(y + d, Y) * Z, Z)],
                rq.at[y],
                b2s.at[kv, d],
                b2r.at[kv, d],
                at_y(d),
            )
            for d in range(1, Y)
        ]

    def reduce_y(kv, rq, u, fin):
        for cp in b2[kv]:
            cp.wait_recv()
        total = rq[0].astype(F32)
        for source in range(1, Y):
            total += rq[source].astype(F32)
        u[...] = total.astype(BF16)
        fin[z] = u[z]
        b1[kv] = [
            send(u.at[lax.rem(z + d, Z)], fin.at[z], b1s.at[kv, d], b1r.at[kv, d], at_z(d))
            for d in range(1, Z)
        ]

    def reduce_end(kv, fin, out, dst):
        for cp in b1[kv]:
            cp.wait_recv()
        out[...] = fin[...].astype(F32)
        stores.append(pltpu.make_async_copy(out, dst, loc.at[17 + kv]))
        stores[-1].start()

    core = [None] * CH
    one = [None] * CH
    two = [None] * CH

    def product(n):
        part = dot(att_s[...], w_s[:, n * CW : (n + 1) * CW])
        pb[n] = part.astype(BF16).reshape(X, 2, 32, CW)
        core[n] = send(pb.at[n, :, 1 - c], rb1.at[n], cs.at[n], cr.at[n], partner)

    def ring_one(n):
        core[n].wait_recv()
        for d in range(X):
            b = lax.rem(x + d, X)
            acc[n, d] = (pb[n, b, c].astype(F32) + rb1[n, b].astype(F32)).astype(BF16)
        one[n] = (
            send(acc.at[n, 2, pl.ds(0, 16)], rs1.at[n, 0], r1s.at[n, 0], r1r.at[n, 0], to_right),
            send(acc.at[n, 2, pl.ds(16, 16)], rs1.at[n, 1], r1s.at[n, 1], r1r.at[n, 1], to_left),
        )

    def ring_two(n):
        one[n][0].wait_recv()
        acc[n, 1, :16] = (acc[n, 1, :16].astype(F32) + rs1[n, 0].astype(F32)).astype(BF16)
        first = send(acc.at[n, 1], rs2.at[n, 0], r2s.at[n, 0], r2r.at[n, 0], to_right)
        one[n][1].wait_recv()
        acc[n, 3, 16:] = (acc[n, 3, 16:].astype(F32) + rs1[n, 1].astype(F32)).astype(BF16)
        two[n] = (
            first,
            send(acc.at[n, 3], rs2.at[n, 1], r2s.at[n, 1], r2r.at[n, 1], to_left),
        )

    def ring_end(n):
        two[n][0].wait_recv()
        two[n][1].wait_recv()
        total = acc[n, 0].astype(F32) + rs2[n, 0].astype(F32) + rs2[n, 1].astype(F32)
        bo_s[:, n * CW : (n + 1) * CW] = total.astype(BF16)

    product(0)
    product(1)
    ring_one(0)
    product(2)
    ring_one(1)
    product(3)
    lax.fori_loop(0, HEADS, query_head, 0, unroll=True)
    stores.append(pltpu.make_async_copy(gq_s, gq_h, loc.at[16]))
    stores[-1].start()
    reduce_z(1, rg_v, qs_v, rq_v)
    ring_one(2)
    ring_one(3)
    ring_two(0)
    reduce_z(0, rg_k, qs_k, rq_k)
    ring_two(1)
    reduce_y(1, rq_v, u_v, fin_v)
    ring_two(2)
    ring_two(3)
    reduce_y(0, rq_k, u_k, fin_k)
    early = len(sent)
    for cp in sent[: early - 2 * Z]:
        cp.wait_send()
    ring_end(0)
    ring_end(1)
    reduce_end(1, fin_v, out_v, gpv_h)
    ring_end(2)
    ring_end(3)
    stores.append(pltpu.make_async_copy(bo_s, bo_h, loc.at[19]))
    stores[-1].start()
    reduce_end(0, fin_k, out_k, gpk_h)
    for cp in sent[early - 2 * Z :]:
        cp.wait_send()
    for cp in stores:
        cp.wait()


def place(*refs):
    ins, outs, held, (taken, given) = refs[:6], refs[6:12], refs[12:18], refs[18:]
    loads = [pltpu.make_async_copy(a, b, taken.at[i]) for i, (a, b) in enumerate(zip(ins, held))]
    stores = [pltpu.make_async_copy(a, b, given.at[i]) for i, (a, b) in enumerate(zip(held, outs))]
    for cp in loads:
        cp.start()
    for load, store in zip(loads, stores):
        load.wait()
        store.start()
    for cp in stores:
        cp.wait()


def local(
    queries, keys, values, prompt_keys, prompt_values,
    lengths, owner_slice, device_group, out_weight, cotangent,
):
    smem = pl.BlockSpec(memory_space=pltpu.SMEM)
    hbm = pl.BlockSpec(memory_space=pl.ANY)
    vm = pltpu.VMEM
    dma = pltpu.SemaphoreType.DMA
    tile = (16, HEAD)
    scratch = [
        vm((HEADS * HEAD, D), BF16),
        vm((X, ROWS, PAIR), BF16),
        vm((HEADS * HEAD, ROWS), F32),
        vm((HEADS, HEAD, ROWS), BF16),
        vm((HEADS, ROWS, HEAD), BF16),
        vm((6, Z) + tile, BF16),
        vm((6, Z) + tile, BF16),
        vm((HEAD, KEYS), BF16),
        vm((HEAD, KEYS), BF16),
        vm((Y * Z,) + tile, BF16),
        vm((Y * Z,) + tile, BF16),
        vm((Z, 4) + tile, BF16),
        vm((Z, 4) + tile, BF16),
        vm((ROWS, ROWS), jnp.int32),
        vm((KEYS, HEADS * ROWS), BF16),
        vm((KEYS, HEADS * ROWS), BF16),
        vm((HEAD, HEADS * ROWS), BF16),
        vm((HEADS, 1, ROWS), F32),
        vm((HEADS, 1, ROWS), F32),
        vm((ROWS, HEADS * HEAD), BF16),
        vm((ROWS, HEADS * HEAD), BF16),
        vm((2, ROWS, HEAD), BF16),
        vm((4, Z) + tile, BF16),
        vm((4, Z) + tile, BF16),
        vm((Z, 4) + tile, BF16),
        vm((Z, 4) + tile, BF16),
        vm((Y * Z,) + tile, BF16),
        vm((Y * Z,) + tile, BF16),
        vm((Y, Z) + tile, BF16),
        vm((Y, Z) + tile, BF16),
        vm((Z,) + tile, BF16),
        vm((Z,) + tile, BF16),
        vm((Z,) + tile, BF16),
        vm((Z,) + tile, BF16),
        vm((Z,) + tile, F32),
        vm((Z,) + tile, F32),
        vm((CH, X, 2, 32, CW), BF16),
        vm((CH, X, 32, CW), BF16),
        vm((CH, X, 32, CW), BF16),
        vm((CH, 2, 16, CW), BF16),
        vm((CH, 2, 32, CW), BF16),
        vm((32, D), BF16),
        pltpu.SMEM((Y * Z,), jnp.int32),
        dma((20,)),
        dma((2, Z)), dma((2, Z)),
        dma((2, Y)), dma((2, Y)),
        dma((2, Z)), dma((2, Z)),
        dma((6,)), dma((6,)),
        dma((7,)), dma((7,)),
        dma((2, Z)), dma((2, Z)),
        dma((2, Y)), dma((2, Y)),
        dma((2, Z)), dma((2, Z)),
        dma((CH,)), dma((CH,)),
        dma((CH, 2)), dma((CH, 2)),
        dma((CH, 2)), dma((CH, 2)),
    ]
    shape = jax.ShapeDtypeStruct
    outs = pl.pallas_call(
        kernel,
        out_shape=(
            shape((32, D), BF16),
            shape((ROWS, HEADS * HEAD), BF16),
            shape((ROWS, HEAD), BF16),
            shape((ROWS, HEAD), BF16),
            shape((Z,) + tile, F32),
            shape((Z,) + tile, F32),
        ),
        in_specs=[smem] * 3 + [hbm] * 7,
        out_specs=[hbm] * 6,
        scratch_shapes=scratch,
        compiler_params=pltpu.CompilerParams(
            collective_id=0, has_side_effects=True, vmem_limit_bytes=58 * 1024 * 1024
        ),
        name="attention_block",
    )(
        lengths,
        owner_slice,
        device_group,
        queries,
        keys.reshape(2, Z, 16, HEAD),
        values.reshape(2, Z, 16, HEAD),
        prompt_keys.reshape(Z, 16, HEAD),
        prompt_values.reshape(Z, 16, HEAD),
        out_weight,
        cotangent,
    )
    outs = pl.pallas_call(
        place,
        out_shape=tuple(shape(o.shape, o.dtype) for o in outs),
        in_specs=[hbm] * 6,
        out_specs=[hbm] * 6,
        scratch_shapes=[vm(o.shape, o.dtype) for o in outs] + [dma((6,)), dma((6,))],
        name="place",
    )(*outs)
    return outs[:4] + (outs[4].reshape(128, HEAD), outs[5].reshape(128, HEAD))


def solution(mesh):
    placed = (
        P("dp", "tensor"),
        P("dp", "tensor"),
        P("dp", "tensor"),
        P("dp", "tensor"),
        P("dp", "tensor"),
        P("dp", None),
        P(),
        P(),
        P("tensor", None),
        P("dp", "tensor"),
    )
    return jax.shard_map(
        local,
        mesh=mesh,
        in_specs=placed,
        out_specs=(
            P(("dp", "tensor"), None),
            P("dp", "tensor"),
            P("dp", "tensor"),
            P("dp", "tensor"),
            P("dp", "tensor"),
            P("dp", "tensor"),
        ),
        check_vma=False,
    )
```

```python
import functools

import jax
import jax.numpy as jnp
from jax import lax
from jax.experimental import pallas as pl
from jax.experimental.pallas import tpu as pltpu
from jax.sharding import PartitionSpec as P

Y, Z, X = 4, 8, 4
HEAD = 128
HEADS = 8
ROWS = 256
PROMPT = 512
KEYS = PROMPT + ROWS
D = 5120
BLK = D // 8
PAIR = 2 * BLK
CH = 4
CW = D // CH
SCALE = HEAD**-0.5
EXP_SCALE = SCALE * 1.4426950408889634
MASKED = -1e30 / SCALE
MESH = pl.DeviceIdType.MESH
F32, BF16 = jnp.float32, jnp.bfloat16
NT = (((1,), (1,)), ((), ()))
NN = (((1,), (0,)), ((), ()))


def dot(a, b, dims=NN):
    return lax.dot_general(a, b, dims, preferred_element_type=F32)


def kernel(
    len_s, own_s, grp_s,
    q_h, k_h, v_h, pk_h, pv_h, w_h, cot_h,
    bo_h, gq_h, gk_h, gv_h, gpk_h, gpv_h,
    pk_s, pv_s, w_s, cot_s, ga_acc, ga_t, q3, kall, vall, kt_s, vt_s, parts_k, parts_v, pick_k, pick_v,
    mask_s, pt_s, ds_s, ga_n, inverse_s, delta_s, att_s, gq_s, gkv_s,
    g_k, g_v, rg_k, rg_v, qs_k, qs_v, rq_k, rq_v, u_k, u_v, so_s, top_s,
    pb, rb1, acc, rs1, rs2, bo_s, inv_s,
    loc, z1s, z1r, y2s, y2r, z3s, z3r, xs, xr, ps, pr,
    b3s, b3r, b2s, b2r, b1s, b1r, cs, cr, r1s, r1r, r2s, r2r,
):
    me = lax.axis_index("dp")
    t = lax.axis_index("tensor")
    y, z = me // Z, me % Z
    x, c = t // 2, t % 2
    right = lax.rem(x + 1, X)
    left = lax.rem(x + X - 1, X)
    opp = lax.rem(x + 2, X)

    def at_z(d):
        return (y * Z + lax.rem(z + d, Z), t)

    def at_y(d):
        return (lax.rem(y + d, Y) * Z + z, t)

    to_right = (me, right * 2 + c)
    to_left = (me, left * 2 + c)
    partner = (me, x * 2 + 1 - c)
    sent = []

    def send(src, dst, ss, rs, dev):
        cp = pltpu.make_async_remote_copy(
            src_ref=src, dst_ref=dst, send_sem=ss, recv_sem=rs, device_id=dev, device_id_type=MESH
        )
        cp.start()
        sent.append(cp)
        return cp

    lane = pl.ds(pl.multiple_of(c * BLK, 128), BLK)
    loads = [
        pltpu.make_async_copy(pk_h, pk_s, loc.at[3]),
        pltpu.make_async_copy(pv_h, pv_s, loc.at[4]),
        pltpu.make_async_copy(cot_h, cot_s.at[x, :, lane], loc.at[0]),
        pltpu.make_async_copy(k_h, kall.at[pl.ds(4, 2)], loc.at[1]),
        pltpu.make_async_copy(v_h, vall.at[pl.ds(4, 2)], loc.at[2]),
        pltpu.make_async_copy(w_h, w_s, loc.at[5]),
    ]
    for h in range(HEADS):
        loads.append(
            pltpu.make_async_copy(q_h.at[:, pl.ds(h * HEAD, HEAD)], q3.at[h], loc.at[6 + h])
        )
    for cp in loads[:3]:
        cp.start()

    barrier = pltpu.get_barrier_semaphore()
    peers = [at_z(d) for d in range(1, Z)] + [at_y(d) for d in range(1, Y)]
    peers += [to_right, to_left, partner]
    for dev in peers:
        pl.semaphore_signal(barrier, inc=1, device_id=dev, device_id_type=MESH)
    pl.semaphore_wait(barrier, len(peers))

    z1 = []
    for kv, (src, dst) in enumerate(((pk_s, parts_k), (pv_s, parts_v))):
        loads[kv].wait()
        z1.append(
            [
                send(src.at[lax.rem(z + d, Z)], dst.at[me], z1s.at[kv, d], z1r.at[kv, d], at_z(d))
                for d in range(1, Z)
            ]
        )
    lo, hi = pl.ds(0, 128), pl.ds(128, 128)
    own_cot = cot_s.at[x]
    loads[2].wait()

    def ring(rows, i, dev):
        ref = own_cot.at[rows, lane]
        return send(ref, ref, xs.at[i], xr.at[i], dev)

    ra = ring(lo, 0, to_right)
    lb = ring(hi, 1, to_left)
    rb = ring(hi, 2, to_right)
    la = ring(lo, 3, to_left)
    p_own = send(own_cot.at[:, lane], own_cot.at[:, lane], ps.at[0], pr.at[0], partner)
    for cp in loads[3:]:
        cp.start()
    parts_k[me] = pk_s[z]
    parts_v[me] = pv_s[z]

    def find(s, _):
        def scan(j, found):
            return jnp.where(own_s[j] == s, j, found)

        inv_s[s] = lax.fori_loop(0, Y * Z, scan, jnp.int32(0), unroll=True)
        return 0

    lax.fori_loop(0, Y * Z, find, 0)

    key_at = lax.broadcasted_iota(jnp.int32, (ROWS, ROWS), 0)
    query_at = lax.broadcasted_iota(jnp.int32, (ROWS, ROWS), 1)
    end0 = len_s[0, 0]
    end1 = end0 + len_s[0, 1]
    end2 = end1 + len_s[0, 2]

    def segment(at):
        return (
            (at >= end0).astype(jnp.int32)
            + (at >= end1).astype(jnp.int32)
            + (at >= end2).astype(jnp.int32)
        )

    seen = (segment(key_at) == segment(query_at)) & (key_at <= query_at)
    mask_s[...] = seen.astype(jnp.int32)

    def forward(block, rows, s):
        ref = cot_s.at[block, rows, lane]
        return send(ref, ref, ps.at[s], pr.at[s], partner)

    def grad_att(block, first=False, last=False):
        cols = pl.ds(pl.multiple_of(block * PAIR, 128), PAIR)
        part = dot(w_s[:, cols], cot_s[block], NT)
        if first:
            ga_acc[...] = part
        elif last:
            ga_t[...] = (ga_acc[...] + part).astype(BF16).reshape(HEADS, HEAD, ROWS)
        else:
            ga_acc[...] += part

    y2 = []
    for kv, ref in enumerate((parts_k, parts_v)):
        for cp in z1[kv]:
            cp.wait_recv()
        rows = ref.at[pl.ds(y * Z, Z)]
        y2.append([send(rows, rows, y2s.at[kv, d], y2r.at[kv, d], at_y(d)) for d in range(1, Y)])

    ra.wait_recv()
    ref = cot_s.at[left, lo, lane]
    fr = send(ref, ref, xs.at[4], xr.at[4], to_right)
    lb.wait_recv()
    ref = cot_s.at[right, hi, lane]
    fl = send(ref, ref, xs.at[5], xr.at[5], to_left)
    p_la = forward(left, lo, 1)
    p_rb = forward(right, hi, 2)

    loads[5].wait()
    p_own.wait_recv()
    grad_att(x, first=True)

    z3 = []
    for kv, (ref, pick, full) in enumerate(((parts_k, pick_k, kall), (parts_v, pick_v, vall))):
        for cp in y2[kv]:
            cp.wait_recv()

        def choose(dest, _, ref=ref, pick=pick):
            first = grp_s[y * Z + dest] * 4
            for p in range(4):
                pick[dest, p] = ref[inv_s[first + p]]
            return 0

        lax.fori_loop(0, Z, choose, 0, unroll=True)
        copies = []
        for d in range(1, Z):
            dest = lax.rem(z + d, Z)
            copies.append(
                send(
                    pick.at[dest], full.at[pl.ds(0, 4), z], z3s.at[kv, d], z3r.at[kv, d], at_z(d)
                )
            )
        for p in range(4):
            full[p, z] = pick[z, p]
        z3.append(copies)

    for cp in loads[3:5] + loads[6:]:
        cp.wait()

    def own_head(h, _):
        own = dot(kall[4:].reshape(ROWS, HEAD), q3[h], NT)
        own = jnp.where(mask_s[...] != 0, own, MASKED)
        so_s[h] = own
        top_s[h] = jnp.max(own, 0, keepdims=True)
        return 0

    rb.wait_recv()
    p_lb = forward(left, hi, 3)
    la.wait_recv()
    p_ra = forward(right, lo, 4)
    p_la.wait_recv()
    p_lb.wait_recv()
    grad_att(left)
    fr.wait_recv()
    p_oa = forward(opp, lo, 5)
    fl.wait_recv()
    p_ob = forward(opp, hi, 6)
    p_rb.wait_recv()
    p_ra.wait_recv()
    grad_att(right)
    lax.fori_loop(0, HEADS, own_head, 0, unroll=True)

    def queries_of(h):
        return pl.ds(pl.multiple_of(h * ROWS, ROWS), ROWS)

    def features_of(h):
        return pl.ds(pl.multiple_of(h * HEAD, HEAD), HEAD)

    for cp in z3[0]:
        cp.wait_recv()

    def score_head(h, _):
        s0 = dot(kall[:4].reshape(PROMPT, HEAD), q3[h], NT)
        top = jnp.maximum(jnp.max(s0, 0, keepdims=True), top_s[h])
        e0 = jnp.exp2((s0 - top) * EXP_SCALE)
        e1 = jnp.exp2((so_s[h] - top) * EXP_SCALE)
        total = jnp.sum(e0, 0, keepdims=True) + jnp.sum(e1, 0, keepdims=True)
        inverse_s[h] = 1.0 / total
        pt_s[:PROMPT, queries_of(h)] = e0.astype(BF16)
        pt_s[PROMPT:, queries_of(h)] = e1.astype(BF16)
        return 0

    lax.fori_loop(0, HEADS, score_head, 0, unroll=True)

    p_oa.wait_recv()
    p_ob.wait_recv()
    grad_att(opp, last=True)

    for cp in z3[1]:
        cp.wait_recv()
    vt_s[...] = vall[...].reshape(KEYS, HEAD).T

    def value_head(h, _):
        inverse = inverse_s[h]
        out_t = dot(vt_s[...], pt_s[:, queries_of(h)]) * inverse
        low = out_t.astype(BF16).astype(F32)
        grad = ga_t[h].astype(F32)
        delta_s[h] = jnp.sum(low * grad, 0, keepdims=True) * inverse
        ga_n[:, queries_of(h)] = (grad * inverse).astype(BF16)
        att_s[:, features_of(h)] = out_t.T.astype(BF16)
        return 0

    lax.fori_loop(0, HEADS, value_head, 0, unroll=True)

    def reduce_start(kv, grad, g_ref, rg):
        g_ref[...] = grad.astype(BF16).reshape(4, Z, 16, HEAD)
        rg[z] = g_ref[:, z]
        return [
            send(
                g_ref.at[:, lax.rem(z + d, Z)], rg.at[z], b3s.at[kv, d], b3r.at[kv, d], at_z(d)
            )
            for d in range(1, Z)
        ]

    b3 = [None, None]
    b2 = [None, None]
    b1 = [None, None]
    stores = []

    def store(src, dst, i):
        stores.append(pltpu.make_async_copy(src, dst, loc.at[i]))
        stores[-1].start()

    def score_grads(rows, values):
        def head(h, _):
            grad_p = dot(values, ga_n[:, queries_of(h)])
            probs = pt_s[rows, queries_of(h)].astype(F32)
            ds_s[rows, queries_of(h)] = (probs * (grad_p - delta_s[h])).astype(BF16)
            return 0

        lax.fori_loop(0, HEADS, head, 0, unroll=True)

    prompt, own = slice(0, PROMPT), slice(PROMPT, KEYS)

    def value_grads(rows):
        return dot(pt_s[rows], ga_n[...], NT)

    def key_grads(rows):
        return dot(ds_s[rows], q3[...].reshape(HEADS * ROWS, HEAD)) * SCALE

    def query_head(h, _):
        dq = dot(kt_s[...], ds_s[:, queries_of(h)])
        gq_s[:, features_of(h)] = (dq.T * SCALE).astype(BF16)
        return 0

    def reduce_z(kv, rg, qs, rq):
        for cp in b3[kv]:
            cp.wait_recv()

        def slot(j, _):
            s = own_s[j]
            group, piece = s // 4, s % 4
            total = jnp.zeros((16, HEAD), F32)
            for source in range(Z):
                hit = jnp.full((16, HEAD), grp_s[y * Z + source], jnp.int32) == group
                total += jnp.where(hit, rg[source, piece].astype(F32), 0.0)
            qs[j] = total.astype(BF16)
            return 0

        lax.fori_loop(0, Y * Z, slot, 0, unroll=4)
        rq[y] = qs[pl.ds(y * Z, Z)]
        b2[kv] = [
            send(
                qs.at[pl.ds(lax.rem(y + d, Y) * Z, Z)],
                rq.at[y],
                b2s.at[kv, d],
                b2r.at[kv, d],
                at_y(d),
            )
            for d in range(1, Y)
        ]

    def reduce_y(kv, rq, u, out):
        for cp in b2[kv]:
            cp.wait_recv()
        total = rq[0].astype(F32)
        for source in range(1, Y):
            total += rq[source].astype(F32)
        u[...] = total.astype(BF16)
        b1[kv] = [
            send(u.at[lax.rem(z + d, Z)], out.at[z], b1s.at[kv, d], b1r.at[kv, d], at_z(d))
            for d in range(1, Z)
        ]
        store(u.at[z], out.at[z], 17 + kv)

    core = [None] * CH
    one = [None] * CH
    two = [None] * CH

    def product(n):
        part = dot(att_s[...], w_s[:, n * CW : (n + 1) * CW])
        pb[n] = part.astype(BF16).reshape(X, 2, 32, CW)
        core[n] = send(pb.at[n, :, 1 - c], rb1.at[n], cs.at[n], cr.at[n], partner)

    def ring_one(n):
        core[n].wait_recv()
        for d in range(X):
            b = lax.rem(x + d, X)
            acc[n, d] = (pb[n, b, c].astype(F32) + rb1[n, b].astype(F32)).astype(BF16)
        one[n] = (
            send(acc.at[n, 2, pl.ds(0, 16)], rs1.at[n, 0], r1s.at[n, 0], r1r.at[n, 0], to_right),
            send(acc.at[n, 2, pl.ds(16, 16)], rs1.at[n, 1], r1s.at[n, 1], r1r.at[n, 1], to_left),
        )

    def ring_two(n):
        one[n][0].wait_recv()
        acc[n, 1, :16] = (acc[n, 1, :16].astype(F32) + rs1[n, 0].astype(F32)).astype(BF16)
        first = send(acc.at[n, 1], rs2.at[n, 0], r2s.at[n, 0], r2r.at[n, 0], to_right)
        one[n][1].wait_recv()
        acc[n, 3, 16:] = (acc[n, 3, 16:].astype(F32) + rs1[n, 1].astype(F32)).astype(BF16)
        two[n] = (
            first,
            send(acc.at[n, 3], rs2.at[n, 1], r2s.at[n, 1], r2r.at[n, 1], to_left),
        )

    def ring_end(n):
        two[n][0].wait_recv()
        two[n][1].wait_recv()
        total = acc[n, 0].astype(F32) + rs2[n, 0].astype(F32) + rs2[n, 1].astype(F32)
        cols = pl.ds(n * CW, CW)
        bo_s[:, cols] = total.astype(BF16)
        store(bo_s.at[:, cols], bo_h.at[:, cols], 19 + n)

    b3[1] = reduce_start(1, value_grads(prompt), g_v, rg_v)
    score_grads(prompt, vall[:4].reshape(PROMPT, HEAD))
    b3[0] = reduce_start(0, key_grads(prompt), g_k, rg_k)
    product(0)
    product(1)
    product(2)
    ring_one(0)
    product(3)
    ring_one(1)
    score_grads(own, vall[4:].reshape(ROWS, HEAD))
    ring_one(2)
    gkv_s[1] = value_grads(own).astype(BF16)
    store(gkv_s.at[1], gv_h, 14)
    kt_s[...] = kall[...].reshape(KEYS, HEAD).T
    ring_one(3)
    reduce_z(1, rg_v, qs_v, rq_v)
    ring_two(0)
    reduce_z(0, rg_k, qs_k, rq_k)
    ring_two(1)
    gkv_s[0] = key_grads(own).astype(BF16)
    store(gkv_s.at[0], gk_h, 15)
    ring_two(2)
    lax.fori_loop(0, HEADS, query_head, 0, unroll=True)
    store(gq_s, gq_h, 16)
    ring_two(3)
    reduce_y(1, rq_v, u_v, gpv_h)
    reduce_y(0, rq_k, u_k, gpk_h)
    ring_end(0)
    ring_end(1)
    late = 2 * Z - 2
    for cp in sent[:-late]:
        cp.wait_send()
    ring_end(2)
    ring_end(3)
    for copies in (b1[1], b1[0]):
        for cp in copies:
            cp.wait_recv()
    for cp in sent[-late:]:
        cp.wait_send()
    for cp in stores:
        cp.wait()


def place(*refs):
    ins, outs, held, wide = refs[:6], refs[6:12], refs[12:18], refs[18:20]
    taken, given = refs[20:]
    loads = [pltpu.make_async_copy(a, b, taken.at[i]) for i, (a, b) in enumerate(zip(ins, held))]
    ready = held[:4] + wide
    stores = [pltpu.make_async_copy(a, b, given.at[i]) for i, (a, b) in enumerate(zip(ready, outs))]
    for cp in loads:
        cp.start()
    for i, (load, store) in enumerate(zip(loads, stores)):
        load.wait()
        if i >= 4:
            wide[i - 4][...] = held[i][...].astype(F32)
        store.start()
    for cp in stores:
        cp.wait()


def local(
    queries, keys, values, prompt_keys, prompt_values,
    lengths, owner_slice, device_group, out_weight, cotangent,
):
    smem = pl.BlockSpec(memory_space=pltpu.SMEM)
    hbm = pl.BlockSpec(memory_space=pl.ANY)
    vm = pltpu.VMEM
    dma = pltpu.SemaphoreType.DMA
    tile = (16, HEAD)
    scratch = [
        vm((Z,) + tile, BF16),
        vm((Z,) + tile, BF16),
        vm((HEADS * HEAD, D), BF16),
        vm((X, ROWS, PAIR), BF16),
        vm((HEADS * HEAD, ROWS), F32),
        vm((HEADS, HEAD, ROWS), BF16),
        vm((HEADS, ROWS, HEAD), BF16),
        vm((6, Z) + tile, BF16),
        vm((6, Z) + tile, BF16),
        vm((HEAD, KEYS), BF16),
        vm((HEAD, KEYS), BF16),
        vm((Y * Z,) + tile, BF16),
        vm((Y * Z,) + tile, BF16),
        vm((Z, 4) + tile, BF16),
        vm((Z, 4) + tile, BF16),
        vm((ROWS, ROWS), jnp.int32),
        vm((KEYS, HEADS * ROWS), BF16),
        vm((KEYS, HEADS * ROWS), BF16),
        vm((HEAD, HEADS * ROWS), BF16),
        vm((HEADS, 1, ROWS), F32),
        vm((HEADS, 1, ROWS), F32),
        vm((ROWS, HEADS * HEAD), BF16),
        vm((ROWS, HEADS * HEAD), BF16),
        vm((2, ROWS, HEAD), BF16),
        vm((4, Z) + tile, BF16),
        vm((4, Z) + tile, BF16),
        vm((Z, 4) + tile, BF16),
        vm((Z, 4) + tile, BF16),
        vm((Y * Z,) + tile, BF16),
        vm((Y * Z,) + tile, BF16),
        vm((Y, Z) + tile, BF16),
        vm((Y, Z) + tile, BF16),
        vm((Z,) + tile, BF16),
        vm((Z,) + tile, BF16),
        vm((HEADS, ROWS, ROWS), F32),
        vm((HEADS, 1, ROWS), F32),
        vm((CH, X, 2, 32, CW), BF16),
        vm((CH, X, 32, CW), BF16),
        vm((CH, X, 32, CW), BF16),
        vm((CH, 2, 16, CW), BF16),
        vm((CH, 2, 32, CW), BF16),
        vm((32, D), BF16),
        pltpu.SMEM((Y * Z,), jnp.int32),
        dma((19 + CH,)),
        dma((2, Z)), dma((2, Z)),
        dma((2, Y)), dma((2, Y)),
        dma((2, Z)), dma((2, Z)),
        dma((6,)), dma((6,)),
        dma((7,)), dma((7,)),
        dma((2, Z)), dma((2, Z)),
        dma((2, Y)), dma((2, Y)),
        dma((2, Z)), dma((2, Z)),
        dma((CH,)), dma((CH,)),
        dma((CH, 2)), dma((CH, 2)),
        dma((CH, 2)), dma((CH, 2)),
    ]
    shape = jax.ShapeDtypeStruct
    outs = pl.pallas_call(
        kernel,
        out_shape=(
            shape((32, D), BF16),
            shape((ROWS, HEADS * HEAD), BF16),
            shape((ROWS, HEAD), BF16),
            shape((ROWS, HEAD), BF16),
            shape((Z,) + tile, BF16),
            shape((Z,) + tile, BF16),
        ),
        in_specs=[smem] * 3 + [hbm] * 7,
        out_specs=[hbm] * 6,
        scratch_shapes=scratch,
        compiler_params=pltpu.CompilerParams(
            collective_id=0, has_side_effects=True, vmem_limit_bytes=58 * 1024 * 1024
        ),
        name="attention_block",
    )(
        lengths,
        owner_slice,
        device_group,
        queries,
        keys.reshape(2, Z, 16, HEAD),
        values.reshape(2, Z, 16, HEAD),
        prompt_keys.reshape(Z, 16, HEAD),
        prompt_values.reshape(Z, 16, HEAD),
        out_weight,
        cotangent,
    )
    wide = shape((Z,) + tile, F32)
    outs = pl.pallas_call(
        place,
        out_shape=tuple(shape(o.shape, o.dtype) for o in outs[:4]) + (wide, wide),
        in_specs=[hbm] * 6,
        out_specs=[hbm] * 6,
        scratch_shapes=[vm(o.shape, o.dtype) for o in outs]
        + [vm(wide.shape, F32)] * 2
        + [dma((6,)), dma((6,))],
        name="place",
    )(*outs)
    return outs[:4] + (outs[4].reshape(128, HEAD), outs[5].reshape(128, HEAD))


def solution(mesh):
    placed = (
        P("dp", "tensor"),
        P("dp", "tensor"),
        P("dp", "tensor"),
        P("dp", "tensor"),
        P("dp", "tensor"),
        P("dp", None),
        P(),
        P(),
        P("tensor", None),
        P("dp", "tensor"),
    )
    return jax.shard_map(
        local,
        mesh=mesh,
        in_specs=placed,
        out_specs=(
            P(("dp", "tensor"), None),
            P("dp", "tensor"),
            P("dp", "tensor"),
            P("dp", "tensor"),
            P("dp", "tensor"),
            P("dp", "tensor"),
        ),
        check_vma=False,
    )
```

```python
import functools

import jax
import jax.numpy as jnp
from jax import lax
from jax.experimental import pallas as pl
from jax.experimental.pallas import tpu as pltpu
from jax.sharding import PartitionSpec as P

Y, Z, X = 4, 8, 4
HEAD = 128
HEADS = 8
ROWS = 256
PROMPT = 512
KEYS = PROMPT + ROWS
D = 5120
BLK = D // 8
PAIR = 2 * BLK
CH = 4
CW = D // CH
SCALE = HEAD**-0.5
EXP_SCALE = SCALE * 1.4426950408889634
MASKED = -1e30 / SCALE
MESH = pl.DeviceIdType.MESH
F32, BF16 = jnp.float32, jnp.bfloat16
NT = (((1,), (1,)), ((), ()))
NN = (((1,), (0,)), ((), ()))


def dot(a, b, dims=NN):
    return lax.dot_general(a, b, dims, preferred_element_type=F32)


def kernel(
    len_s, own_s, grp_s,
    q_h, k_h, v_h, pk_h, pv_h, w_h, cot_h,
    bo_h, gq_h, gk_h, gv_h, gpk_h, gpv_h,
    pk_s, pv_s, w_s, cot_s, ga_acc, ga_t, q_s, q3, kall, vall, kt_s, vt_s, parts_k, parts_v, pick_k, pick_v,
    mask_s, pt_s, ds_s, ga_n, inverse_s, delta_s, att_s, gq_s, gkv_s,
    g_k, g_v, rg_k, rg_v, qs_k, qs_v, rq_k, rq_v, u_k, u_v, so_s, top_s,
    pb, rb1, acc, rs1, rs2, bo_s, inv_s,
    loc, zs, zr, xs, xr, ps, pr, cs, cr, r1s, r1r, r2s, r2r,
):
    me = lax.axis_index("dp")
    t = lax.axis_index("tensor")
    y, z = me // Z, me % Z
    x, c = t // 2, t % 2
    right = lax.rem(x + 1, X)
    left = lax.rem(x + X - 1, X)
    opp = lax.rem(x + 2, X)

    def at_z(d):
        return (y * Z + lax.rem(z + d, Z), t)

    def at_y(d):
        return (lax.rem(y + d, Y) * Z + z, t)

    to_right = (me, right * 2 + c)
    to_left = (me, left * 2 + c)
    partner = (me, x * 2 + 1 - c)

    def send(src, dst, ss, rs, dev):
        cp = pltpu.make_async_remote_copy(
            src_ref=src, dst_ref=dst, send_sem=ss, recv_sem=rs, device_id=dev, device_id_type=MESH
        )
        cp.start()
        return cp

    def arrived(ref, rs):
        pltpu.make_async_remote_copy(
            src_ref=ref, dst_ref=ref, send_sem=rs, recv_sem=rs, device_id=partner,
            device_id_type=MESH,
        ).wait_recv()

    def left_here(ref, ss):
        pltpu.make_async_remote_copy(
            src_ref=ref, dst_ref=ref, send_sem=ss, recv_sem=ss, device_id=partner,
            device_id_type=MESH,
        ).wait_send()

    lane = pl.ds(pl.multiple_of(c * BLK, 128), BLK)
    loads = [
        pltpu.make_async_copy(pk_h, pk_s, loc.at[3]),
        pltpu.make_async_copy(pv_h, pv_s, loc.at[4]),
        pltpu.make_async_copy(cot_h, cot_s.at[x, :, lane], loc.at[0]),
        pltpu.make_async_copy(k_h, kall.at[pl.ds(4, 2)], loc.at[1]),
        pltpu.make_async_copy(v_h, vall.at[pl.ds(4, 2)], loc.at[2]),
        pltpu.make_async_copy(q_h, q_s, loc.at[6]),
        pltpu.make_async_copy(w_h, w_s, loc.at[5]),
    ]
    for cp in loads[:3]:
        cp.start()

    barrier = pltpu.get_barrier_semaphore()
    peers = [at_z(d) for d in range(1, Z)] + [at_y(d) for d in range(1, Y)]
    peers += [to_right, to_left, partner]
    for dev in peers:
        pl.semaphore_signal(barrier, inc=1, device_id=dev, device_id_type=MESH)
    pl.semaphore_wait(barrier, len(peers))

    for kv, (src, dst) in enumerate(((pk_s, parts_k), (pv_s, parts_v))):
        loads[kv].wait()
        for d in range(1, Z):
            send(src.at[lax.rem(z + d, Z)], dst.at[me], zs.at[0, kv], zr.at[0, kv], at_z(d))
    lo, hi = pl.ds(0, 128), pl.ds(128, 128)
    own_cot = cot_s.at[x]
    loads[2].wait()

    def ring(rows, i, dev):
        ref = own_cot.at[rows, lane]
        return send(ref, ref, xs.at[0], xr.at[i], dev)

    ra = ring(lo, 0, to_right)
    lb = ring(hi, 1, to_left)
    rb = ring(hi, 2, to_right)
    la = ring(lo, 3, to_left)
    p_own = send(own_cot.at[:, lane], own_cot.at[:, lane], ps.at[0], pr.at[0], partner)
    for cp in loads[3:]:
        cp.start()
    parts_k[me] = pk_s[z]
    parts_v[me] = pv_s[z]

    def find(s, _):
        def scan(j, found):
            return jnp.where(own_s[j] == s, j, found)

        inv_s[s] = lax.fori_loop(0, Y * Z, scan, jnp.int32(0), unroll=True)
        return 0

    lax.fori_loop(0, Y * Z, find, 0)

    key_at = lax.broadcasted_iota(jnp.int32, (ROWS, ROWS), 0)
    query_at = lax.broadcasted_iota(jnp.int32, (ROWS, ROWS), 1)
    end0 = len_s[0, 0]
    end1 = end0 + len_s[0, 1]
    end2 = end1 + len_s[0, 2]

    def segment(at):
        return (
            (at >= end0).astype(jnp.int32)
            + (at >= end1).astype(jnp.int32)
            + (at >= end2).astype(jnp.int32)
        )

    seen = (segment(key_at) == segment(query_at)) & (key_at <= query_at)
    mask_s[...] = seen.astype(jnp.int32)

    def forward(block, rows, s):
        ref = cot_s.at[block, rows, lane]
        return send(ref, ref, ps.at[0], pr.at[s], partner)

    def grad_att(block, first=False, last=False):
        cols = pl.ds(pl.multiple_of(block * PAIR, 128), PAIR)
        part = dot(w_s[:, cols], cot_s[block], NT)
        if first:
            ga_acc[...] = part
        elif last:
            ga_t[...] = (ga_acc[...] + part).astype(BF16).reshape(HEADS, HEAD, ROWS)
        else:
            ga_acc[...] += part

    for kv, ref in enumerate((parts_k, parts_v)):
        arrived(ref.at[pl.ds(0, Z - 1)], zr.at[0, kv])
        rows = ref.at[pl.ds(y * Z, Z)]
        for d in range(1, Y):
            send(rows, rows, zs.at[1, kv], zr.at[1, kv], at_y(d))

    ra.wait_recv()
    ref = cot_s.at[left, lo, lane]
    fr = send(ref, ref, xs.at[0], xr.at[4], to_right)
    lb.wait_recv()
    ref = cot_s.at[right, hi, lane]
    fl = send(ref, ref, xs.at[0], xr.at[5], to_left)
    p_la = forward(left, lo, 1)
    p_rb = forward(right, hi, 2)

    loads[6].wait()
    p_own.wait_recv()
    grad_att(x, first=True)

    for kv, (ref, pick, full) in enumerate(((parts_k, pick_k, kall), (parts_v, pick_v, vall))):
        arrived(ref.at[pl.ds(0, (Y - 1) * Z)], zr.at[1, kv])

        def choose(dest, _, ref=ref, pick=pick):
            first = grp_s[y * Z + dest] * 4
            for p in range(4):
                pick[dest, p] = ref[inv_s[first + p]]
            return 0

        lax.fori_loop(0, Z, choose, 0, unroll=True)
        for d in range(1, Z):
            dest = lax.rem(z + d, Z)
            send(pick.at[dest], full.at[pl.ds(0, 4), z], zs.at[2, kv], zr.at[2, kv], at_z(d))
        for p in range(4):
            full[p, z] = pick[z, p]

    for cp in loads[3:6]:
        cp.wait()
    for h in range(HEADS):
        q3[h] = q_s[:, h * HEAD : (h + 1) * HEAD]

    def own_head(h, _):
        own = dot(kall[4:].reshape(ROWS, HEAD), q3[h], NT)
        own = jnp.where(mask_s[...] != 0, own, MASKED)
        so_s[h] = own
        top_s[h] = jnp.max(own, 0, keepdims=True)
        return 0

    rb.wait_recv()
    p_lb = forward(left, hi, 3)
    la.wait_recv()
    p_ra = forward(right, lo, 4)
    p_la.wait_recv()
    p_lb.wait_recv()
    grad_att(left)
    fr.wait_recv()
    p_oa = forward(opp, lo, 5)
    fl.wait_recv()
    p_ob = forward(opp, hi, 6)
    p_rb.wait_recv()
    p_ra.wait_recv()
    grad_att(right)
    lax.fori_loop(0, HEADS, own_head, 0, unroll=True)

    def queries_of(h):
        return pl.ds(pl.multiple_of(h * ROWS, ROWS), ROWS)

    def features_of(h):
        return pl.ds(pl.multiple_of(h * HEAD, HEAD), HEAD)

    arrived(kall.at[pl.ds(0, 4), pl.ds(0, Z - 1)], zr.at[2, 0])

    def score_head(h, _):
        s0 = dot(kall[:4].reshape(PROMPT, HEAD), q3[h], NT)
        top = jnp.maximum(jnp.max(s0, 0, keepdims=True), top_s[h])
        e0 = jnp.exp2((s0 - top) * EXP_SCALE)
        e1 = jnp.exp2((so_s[h] - top) * EXP_SCALE)
        total = jnp.sum(e0, 0, keepdims=True) + jnp.sum(e1, 0, keepdims=True)
        inverse_s[h] = 1.0 / total
        pt_s[:PROMPT, queries_of(h)] = e0.astype(BF16)
        pt_s[PROMPT:, queries_of(h)] = e1.astype(BF16)
        return 0

    lax.fori_loop(0, HEADS, score_head, 0, unroll=True)

    p_oa.wait_recv()
    p_ob.wait_recv()
    grad_att(opp, last=True)

    arrived(vall.at[pl.ds(0, 4), pl.ds(0, Z - 1)], zr.at[2, 1])
    vt_s[...] = vall[...].reshape(KEYS, HEAD).T

    def value_head(h, _):
        inverse = inverse_s[h]
        out_t = dot(vt_s[...], pt_s[:, queries_of(h)]) * inverse
        low = out_t.astype(BF16).astype(F32)
        grad = ga_t[h].astype(F32)
        delta_s[h] = jnp.sum(low * grad, 0, keepdims=True) * inverse
        ga_n[:, queries_of(h)] = (grad * inverse).astype(BF16)
        att_s[:, features_of(h)] = out_t.T.astype(BF16)
        return 0

    lax.fori_loop(0, HEADS, value_head, 0, unroll=True)

    def reduce_start(kv, grad, g_ref, rg):
        g_ref[...] = grad.astype(BF16).reshape(4, Z, 16, HEAD)
        rg[z] = g_ref[:, z]
        for d in range(1, Z):
            send(g_ref.at[:, lax.rem(z + d, Z)], rg.at[z], zs.at[3, kv], zr.at[3, kv], at_z(d))

    stores = []

    def store(src, dst, i):
        stores.append(pltpu.make_async_copy(src, dst, loc.at[i]))
        stores[-1].start()

    def score_grads(rows, values):
        def head(h, _):
            grad_p = dot(values, ga_n[:, queries_of(h)])
            probs = pt_s[rows, queries_of(h)].astype(F32)
            ds_s[rows, queries_of(h)] = (probs * (grad_p - delta_s[h])).astype(BF16)
            return 0

        lax.fori_loop(0, HEADS, head, 0, unroll=True)

    prompt, own = slice(0, PROMPT), slice(PROMPT, KEYS)

    def value_grads(rows):
        return dot(pt_s[rows], ga_n[...], NT)

    def key_grads(rows):
        return dot(ds_s[rows], q3[...].reshape(HEADS * ROWS, HEAD)) * SCALE

    def query_head(h, _):
        dq = dot(kt_s[...], ds_s[:, queries_of(h)])
        gq_s[:, features_of(h)] = (dq.T * SCALE).astype(BF16)
        return 0

    def reduce_z(kv, rg, qs, rq):
        arrived(rg.at[pl.ds(0, Z - 1)], zr.at[3, kv])

        def slot(j, _):
            s = own_s[j]
            group, piece = s // 4, s % 4
            total = jnp.zeros((16, HEAD), F32)
            for source in range(Z):
                hit = jnp.full((16, HEAD), grp_s[y * Z + source], jnp.int32) == group
                total += jnp.where(hit, rg[source, piece].astype(F32), 0.0)
            qs[j] = total.astype(BF16)
            return 0

        lax.fori_loop(0, Y * Z, slot, 0, unroll=4)
        rq[y] = qs[pl.ds(y * Z, Z)]
        for d in range(1, Y):
            block = qs.at[pl.ds(lax.rem(y + d, Y) * Z, Z)]
            send(block, rq.at[y], zs.at[4, kv], zr.at[4, kv], at_y(d))

    def reduce_y(kv, rq, u, out):
        arrived(rq.at[pl.ds(0, Y - 1)], zr.at[4, kv])
        total = rq[0].astype(F32)
        for source in range(1, Y):
            total += rq[source].astype(F32)
        u[...] = total.astype(BF16)
        for d in range(1, Z):
            send(u.at[lax.rem(z + d, Z)], out.at[z], zs.at[5, kv], zr.at[5, kv], at_z(d))
        store(u.at[z], out.at[z], 10 + kv)

    core = [None] * CH
    one = [None] * CH
    two = [None] * CH

    def product(n):
        part = dot(att_s[...], w_s[:, n * CW : (n + 1) * CW])
        pb[n] = part.astype(BF16).reshape(X, 2, 32, CW)
        core[n] = send(pb.at[n, :, 1 - c], rb1.at[n], cs.at[0], cr.at[n], partner)

    def ring_one(n):
        core[n].wait_recv()
        for d in range(X):
            b = lax.rem(x + d, X)
            acc[n, d] = (pb[n, b, c].astype(F32) + rb1[n, b].astype(F32)).astype(BF16)
        one[n] = (
            send(acc.at[n, 2, pl.ds(0, 16)], rs1.at[n, 0], r1s.at[0], r1r.at[n, 0], to_right),
            send(acc.at[n, 2, pl.ds(16, 16)], rs1.at[n, 1], r1s.at[0], r1r.at[n, 1], to_left),
        )

    def ring_two(n):
        one[n][0].wait_recv()
        acc[n, 1, :16] = (acc[n, 1, :16].astype(F32) + rs1[n, 0].astype(F32)).astype(BF16)
        first = send(acc.at[n, 1], rs2.at[n, 0], r2s.at[0], r2r.at[n, 0], to_right)
        one[n][1].wait_recv()
        acc[n, 3, 16:] = (acc[n, 3, 16:].astype(F32) + rs1[n, 1].astype(F32)).astype(BF16)
        two[n] = (
            first,
            send(acc.at[n, 3], rs2.at[n, 1], r2s.at[0], r2r.at[n, 1], to_left),
        )

    def ring_end(n):
        two[n][0].wait_recv()
        two[n][1].wait_recv()
        total = acc[n, 0].astype(F32) + rs2[n, 0].astype(F32) + rs2[n, 1].astype(F32)
        cols = pl.ds(n * CW, CW)
        bo_s[:, cols] = total.astype(BF16)
        store(bo_s.at[:, cols], bo_h.at[:, cols], 12 + n)

    reduce_start(1, value_grads(prompt), g_v, rg_v)
    score_grads(prompt, vall[:4].reshape(PROMPT, HEAD))
    reduce_start(0, key_grads(prompt), g_k, rg_k)
    product(0)
    product(1)
    product(2)
    ring_one(0)
    product(3)
    ring_one(1)
    score_grads(own, vall[4:].reshape(ROWS, HEAD))
    ring_one(2)
    gkv_s[1] = value_grads(own).astype(BF16)
    store(gkv_s.at[1], gv_h, 7)
    kt_s[...] = kall[...].reshape(KEYS, HEAD).T
    ring_one(3)
    reduce_z(1, rg_v, qs_v, rq_v)
    ring_two(0)
    reduce_z(0, rg_k, qs_k, rq_k)
    ring_two(1)
    gkv_s[0] = key_grads(own).astype(BF16)
    store(gkv_s.at[0], gk_h, 8)
    ring_two(2)
    lax.fori_loop(0, HEADS, query_head, 0, unroll=True)
    store(gq_s, gq_h, 9)
    ring_two(3)
    reduce_y(1, rq_v, u_v, gpv_h)
    reduce_y(0, rq_k, u_k, gpk_h)
    ring_end(0)
    ring_end(1)
    for kv in range(2):
        left_here(parts_k.at[pl.ds(0, Z - 1)], zs.at[0, kv])
        left_here(parts_k.at[pl.ds(0, (Y - 1) * Z)], zs.at[1, kv])
        left_here(pick_k.at[pl.ds(0, Z - 1)], zs.at[2, kv])
        left_here(rg_k.at[pl.ds(0, Z - 1)], zs.at[3, kv])
        left_here(rq_k.at[pl.ds(0, Y - 1)], zs.at[4, kv])
    left_here(cot_s.at[pl.ds(0, 3), :, pl.ds(0, BLK)], xs.at[0])
    left_here(cot_s.at[:, :, pl.ds(0, BLK)], ps.at[0])
    left_here(rb1, cs.at[0])
    left_here(rs1, r1s.at[0])
    ring_end(2)
    ring_end(3)
    left_here(rs2, r2s.at[0])
    for kv, (u, out) in ((1, (u_v, gpv_h)), (0, (u_k, gpk_h))):
        arrived(out.at[pl.ds(0, Z - 1)], zr.at[5, kv])
        left_here(u.at[pl.ds(0, Z - 1)], zs.at[5, kv])
    for cp in stores:
        cp.wait()


def place(*refs):
    ins, outs, held, wide = refs[:6], refs[6:12], refs[12:18], refs[18:20]
    taken, given = refs[20:]
    loads = [pltpu.make_async_copy(a, b, taken.at[i]) for i, (a, b) in enumerate(zip(ins, held))]
    ready = held[:4] + wide
    stores = [pltpu.make_async_copy(a, b, given.at[i]) for i, (a, b) in enumerate(zip(ready, outs))]
    for cp in loads:
        cp.start()
    for i, (load, store) in enumerate(zip(loads, stores)):
        load.wait()
        if i >= 4:
            wide[i - 4][...] = held[i][...].astype(F32)
        store.start()
    for cp in stores:
        cp.wait()


def local(
    queries, keys, values, prompt_keys, prompt_values,
    lengths, owner_slice, device_group, out_weight, cotangent,
):
    smem = pl.BlockSpec(memory_space=pltpu.SMEM)
    hbm = pl.BlockSpec(memory_space=pl.ANY)
    vm = pltpu.VMEM
    dma = pltpu.SemaphoreType.DMA
    tile = (16, HEAD)
    scratch = [
        vm((Z,) + tile, BF16),
        vm((Z,) + tile, BF16),
        vm((HEADS * HEAD, D), BF16),
        vm((X, ROWS, PAIR), BF16),
        vm((HEADS * HEAD, ROWS), F32),
        vm((HEADS, HEAD, ROWS), BF16),
        vm((ROWS, HEADS * HEAD), BF16),
        vm((HEADS, ROWS, HEAD), BF16),
        vm((6, Z) + tile, BF16),
        vm((6, Z) + tile, BF16),
        vm((HEAD, KEYS), BF16),
        vm((HEAD, KEYS), BF16),
        vm((Y * Z,) + tile, BF16),
        vm((Y * Z,) + tile, BF16),
        vm((Z, 4) + tile, BF16),
        vm((Z, 4) + tile, BF16),
        vm((ROWS, ROWS), jnp.int32),
        vm((KEYS, HEADS * ROWS), BF16),
        vm((KEYS, HEADS * ROWS), BF16),
        vm((HEAD, HEADS * ROWS), BF16),
        vm((HEADS, 1, ROWS), F32),
        vm((HEADS, 1, ROWS), F32),
        vm((ROWS, HEADS * HEAD), BF16),
        vm((ROWS, HEADS * HEAD), BF16),
        vm((2, ROWS, HEAD), BF16),
        vm((4, Z) + tile, BF16),
        vm((4, Z) + tile, BF16),
        vm((Z, 4) + tile, BF16),
        vm((Z, 4) + tile, BF16),
        vm((Y * Z,) + tile, BF16),
        vm((Y * Z,) + tile, BF16),
        vm((Y, Z) + tile, BF16),
        vm((Y, Z) + tile, BF16),
        vm((Z,) + tile, BF16),
        vm((Z,) + tile, BF16),
        vm((HEADS, ROWS, ROWS), F32),
        vm((HEADS, 1, ROWS), F32),
        vm((CH, X, 2, 32, CW), BF16),
        vm((CH, X, 32, CW), BF16),
        vm((CH, X, 32, CW), BF16),
        vm((CH, 2, 16, CW), BF16),
        vm((CH, 2, 32, CW), BF16),
        vm((32, D), BF16),
        pltpu.SMEM((Y * Z,), jnp.int32),
        dma((16,)),
        dma((6, 2)), dma((6, 2)),
        dma((1,)), dma((6,)),
        dma((1,)), dma((7,)),
        dma((1,)), dma((CH,)),
        dma((1,)), dma((CH, 2)),
        dma((1,)), dma((CH, 2)),
    ]
    shape = jax.ShapeDtypeStruct
    outs = pl.pallas_call(
        kernel,
        out_shape=(
            shape((32, D), BF16),
            shape((ROWS, HEADS * HEAD), BF16),
            shape((ROWS, HEAD), BF16),
            shape((ROWS, HEAD), BF16),
            shape((Z,) + tile, BF16),
            shape((Z,) + tile, BF16),
        ),
        in_specs=[smem] * 3 + [hbm] * 7,
        out_specs=[hbm] * 6,
        scratch_shapes=scratch,
        compiler_params=pltpu.CompilerParams(
            collective_id=0, has_side_effects=True, vmem_limit_bytes=58 * 1024 * 1024
        ),
        name="attention_block",
    )(
        lengths,
        owner_slice,
        device_group,
        queries,
        keys.reshape(2, Z, 16, HEAD),
        values.reshape(2, Z, 16, HEAD),
        prompt_keys.reshape(Z, 16, HEAD),
        prompt_values.reshape(Z, 16, HEAD),
        out_weight,
        cotangent,
    )
    wide = shape((Z,) + tile, F32)
    outs = pl.pallas_call(
        place,
        out_shape=tuple(shape(o.shape, o.dtype) for o in outs[:4]) + (wide, wide),
        in_specs=[hbm] * 6,
        out_specs=[hbm] * 6,
        scratch_shapes=[vm(o.shape, o.dtype) for o in outs]
        + [vm(wide.shape, F32)] * 2
        + [dma((6,)), dma((6,))],
        name="place",
    )(*outs)
    return outs[:4] + (outs[4].reshape(128, HEAD), outs[5].reshape(128, HEAD))


def solution(mesh):
    placed = (
        P("dp", "tensor"),
        P("dp", "tensor"),
        P("dp", "tensor"),
        P("dp", "tensor"),
        P("dp", "tensor"),
        P("dp", None),
        P(),
        P(),
        P("tensor", None),
        P("dp", "tensor"),
    )
    return jax.shard_map(
        local,
        mesh=mesh,
        in_specs=placed,
        out_specs=(
            P(("dp", "tensor"), None),
            P("dp", "tensor"),
            P("dp", "tensor"),
            P("dp", "tensor"),
            P("dp", "tensor"),
            P("dp", "tensor"),
        ),
        check_vma=False,
    )
```

```python
import functools

import jax
import jax.numpy as jnp
from jax import lax
from jax.experimental import pallas as pl
from jax.experimental.pallas import tpu as pltpu
from jax.sharding import PartitionSpec as P

Y, Z, X = 4, 8, 4
HEAD = 128
HEADS = 8
ROWS = 256
PROMPT = 512
KEYS = PROMPT + ROWS
D = 5120
BLK = D // 8
PAIR = 2 * BLK
CH = 4
CW = D // CH
SCALE = HEAD**-0.5
EXP_SCALE = SCALE * 1.4426950408889634
MASKED = -1e30 / SCALE
MESH = pl.DeviceIdType.MESH
F32, BF16 = jnp.float32, jnp.bfloat16
NT = (((1,), (1,)), ((), ()))
NN = (((1,), (0,)), ((), ()))


def dot(a, b, dims=NN):
    return lax.dot_general(a, b, dims, preferred_element_type=F32)


def kernel(
    len_s, own_s, grp_s,
    q_h, k_h, v_h, pk_h, pv_h, w_h, cot_h,
    bo_h, gq_h, gk_h, gv_h, gpk_h, gpv_h,
    pk_s, pv_s, w_s, cot_s, ga_acc, ga_t, q_s, q3, kall, vall, kt_s, vt_s, parts_k, parts_v, pick_k, pick_v,
    mask_s, pt_s, ds_s, ga_n, inverse_s, delta_s, att_s, gq_s, gkv_s,
    g_k, g_v, rg_k, rg_v, qs_k, qs_v, rq_k, rq_v, u_k, u_v, so_s, top_s,
    pb, rb1, acc, rs1, rs2, bo_s, inv_s,
    loc, zs, zr, xs, xr, ps, pr, cs, cr, r1s, r1r, r2s, r2r,
):
    me = lax.axis_index("dp")
    t = lax.axis_index("tensor")
    y, z = me // Z, me % Z
    x, c = t // 2, t % 2
    right = lax.rem(x + 1, X)
    left = lax.rem(x + X - 1, X)
    opp = lax.rem(x + 2, X)

    def at_z(d):
        return (y * Z + lax.rem(z + d, Z), t)

    def at_y(d):
        return (lax.rem(y + d, Y) * Z + z, t)

    to_right = (me, right * 2 + c)
    to_left = (me, left * 2 + c)
    partner = (me, x * 2 + 1 - c)

    def send(src, dst, ss, rs, dev):
        cp = pltpu.make_async_remote_copy(
            src_ref=src, dst_ref=dst, send_sem=ss, recv_sem=rs, device_id=dev, device_id_type=MESH
        )
        cp.start()
        return cp

    def arrived(ref, rs):
        pltpu.make_async_remote_copy(
            src_ref=ref, dst_ref=ref, send_sem=rs, recv_sem=rs, device_id=partner,
            device_id_type=MESH,
        ).wait_recv()

    def left_here(ref, ss):
        pltpu.make_async_remote_copy(
            src_ref=ref, dst_ref=ref, send_sem=ss, recv_sem=ss, device_id=partner,
            device_id_type=MESH,
        ).wait_send()

    lane = pl.ds(pl.multiple_of(c * BLK, 128), BLK)
    loads = [
        pltpu.make_async_copy(pk_h, pk_s, loc.at[3]),
        pltpu.make_async_copy(pv_h, pv_s, loc.at[4]),
        pltpu.make_async_copy(cot_h, cot_s.at[x, :, lane], loc.at[0]),
        pltpu.make_async_copy(k_h, kall.at[pl.ds(4, 2)], loc.at[1]),
        pltpu.make_async_copy(v_h, vall.at[pl.ds(4, 2)], loc.at[2]),
        pltpu.make_async_copy(q_h, q_s, loc.at[6]),
        pltpu.make_async_copy(w_h, w_s, loc.at[5]),
    ]
    for cp in loads[:3]:
        cp.start()

    barrier = pltpu.get_barrier_semaphore()
    peers = [at_z(d) for d in range(1, Z)] + [at_y(d) for d in range(1, Y)]
    peers += [to_right, to_left, partner]
    for dev in peers:
        pl.semaphore_signal(barrier, inc=1, device_id=dev, device_id_type=MESH)
    pl.semaphore_wait(barrier, len(peers))

    for kv, (src, dst) in enumerate(((pk_s, parts_k), (pv_s, parts_v))):
        loads[kv].wait()
        for d in range(1, Z):
            send(src.at[lax.rem(z + d, Z)], dst.at[me], zs.at[0, kv], zr.at[0, kv], at_z(d))
    lo, hi = pl.ds(0, 128), pl.ds(128, 128)
    own_cot = cot_s.at[x]
    loads[2].wait()

    def ring(rows, i, dev):
        ref = own_cot.at[rows, lane]
        return send(ref, ref, xs.at[0], xr.at[i], dev)

    ra = ring(lo, 0, to_right)
    lb = ring(hi, 1, to_left)
    rb = ring(hi, 2, to_right)
    la = ring(lo, 3, to_left)
    p_own = send(own_cot.at[:, lane], own_cot.at[:, lane], ps.at[0], pr.at[0], partner)
    for cp in loads[3:]:
        cp.start()
    parts_k[me] = pk_s[z]
    parts_v[me] = pv_s[z]

    def find(s, _):
        def scan(j, found):
            return jnp.where(own_s[j] == s, j, found)

        inv_s[s] = lax.fori_loop(0, Y * Z, scan, jnp.int32(0), unroll=True)
        return 0

    lax.fori_loop(0, Y * Z, find, 0)

    key_at = lax.broadcasted_iota(jnp.int32, (ROWS, ROWS), 0)
    query_at = lax.broadcasted_iota(jnp.int32, (ROWS, ROWS), 1)
    end0 = len_s[0, 0]
    end1 = end0 + len_s[0, 1]
    end2 = end1 + len_s[0, 2]

    def segment(at):
        return (
            (at >= end0).astype(jnp.int32)
            + (at >= end1).astype(jnp.int32)
            + (at >= end2).astype(jnp.int32)
        )

    seen = (segment(key_at) == segment(query_at)) & (key_at <= query_at)
    mask_s[...] = seen.astype(jnp.int32)

    def forward(block, rows, s):
        ref = cot_s.at[block, rows, lane]
        return send(ref, ref, ps.at[0], pr.at[s], partner)

    def grad_att(block, first=False, last=False):
        cols = pl.ds(pl.multiple_of(block * PAIR, 128), PAIR)

        def step(i, _):
            rows = pl.ds(pl.multiple_of(i * 512, 512), 512)
            part = dot(w_s[rows, cols], cot_s[block], NT)
            if first:
                ga_acc[rows, :] = part
            elif last:
                ga_t[pl.ds(i * 4, 4)] = (
                    (ga_acc[rows, :] + part).astype(BF16).reshape(HEADS // 2, HEAD, ROWS)
                )
            else:
                ga_acc[rows, :] += part
            return 0

        lax.fori_loop(0, 2, step, 0)

    for kv, ref in enumerate((parts_k, parts_v)):
        arrived(ref.at[pl.ds(0, Z - 1)], zr.at[0, kv])
        rows = ref.at[pl.ds(y * Z, Z)]
        for d in range(1, Y):
            send(rows, rows, zs.at[1, kv], zr.at[1, kv], at_y(d))

    ra.wait_recv()
    ref = cot_s.at[left, lo, lane]
    fr = send(ref, ref, xs.at[0], xr.at[4], to_right)
    lb.wait_recv()
    ref = cot_s.at[right, hi, lane]
    fl = send(ref, ref, xs.at[0], xr.at[5], to_left)
    p_la = forward(left, lo, 1)
    p_rb = forward(right, hi, 2)

    loads[6].wait()
    p_own.wait_recv()
    grad_att(x, first=True)

    for kv, (ref, pick, full) in enumerate(((parts_k, pick_k, kall), (parts_v, pick_v, vall))):
        arrived(ref.at[pl.ds(0, (Y - 1) * Z)], zr.at[1, kv])

        def choose(dest, _, ref=ref, pick=pick):
            first = grp_s[y * Z + dest] * 4
            for p in range(4):
                pick[dest, p] = ref[inv_s[first + p]]
            return 0

        lax.fori_loop(0, Z, choose, 0, unroll=4)
        for d in range(1, Z):
            dest = lax.rem(z + d, Z)
            send(pick.at[dest], full.at[pl.ds(0, 4), z], zs.at[2, kv], zr.at[2, kv], at_z(d))
        for p in range(4):
            full[p, z] = pick[z, p]

    for cp in loads[3:6]:
        cp.wait()
    for h in range(HEADS):
        q3[h] = q_s[:, h * HEAD : (h + 1) * HEAD]

    def own_head(h, _):
        own = dot(kall[4:].reshape(ROWS, HEAD), q3[h], NT)
        own = jnp.where(mask_s[...] != 0, own, MASKED)
        so_s[h] = own
        top_s[h] = jnp.max(own, 0, keepdims=True)
        return 0

    lax.fori_loop(0, HEADS, own_head, 0, unroll=4)
    rb.wait_recv()
    p_lb = forward(left, hi, 3)
    la.wait_recv()
    p_ra = forward(right, lo, 4)
    p_la.wait_recv()
    p_lb.wait_recv()
    grad_att(left)
    fr.wait_recv()
    p_oa = forward(opp, lo, 5)
    fl.wait_recv()
    p_ob = forward(opp, hi, 6)
    p_rb.wait_recv()
    p_ra.wait_recv()
    grad_att(right)
    def queries_of(h):
        return pl.ds(pl.multiple_of(h * ROWS, ROWS), ROWS)

    def features_of(h):
        return pl.ds(pl.multiple_of(h * HEAD, HEAD), HEAD)

    arrived(kall.at[pl.ds(0, 4), pl.ds(0, Z - 1)], zr.at[2, 0])

    def score_head(h, _):
        s0 = dot(kall[:4].reshape(PROMPT, HEAD), q3[h], NT)
        top = jnp.maximum(jnp.max(s0, 0, keepdims=True), top_s[h])
        e0 = jnp.exp2((s0 - top) * EXP_SCALE)
        e1 = jnp.exp2((so_s[h] - top) * EXP_SCALE)
        total = jnp.sum(e0, 0, keepdims=True) + jnp.sum(e1, 0, keepdims=True)
        inverse_s[h] = 1.0 / total
        pt_s[:PROMPT, queries_of(h)] = e0.astype(BF16)
        pt_s[PROMPT:, queries_of(h)] = e1.astype(BF16)
        return 0

    lax.fori_loop(0, HEADS, score_head, 0, unroll=4)

    p_oa.wait_recv()
    p_ob.wait_recv()
    grad_att(opp, last=True)

    arrived(vall.at[pl.ds(0, 4), pl.ds(0, Z - 1)], zr.at[2, 1])
    vt_s[...] = vall[...].reshape(KEYS, HEAD).T

    def value_head(h, _):
        inverse = inverse_s[h]
        out_t = dot(vt_s[...], pt_s[:, queries_of(h)]) * inverse
        low = out_t.astype(BF16).astype(F32)
        grad = ga_t[h].astype(F32)
        delta_s[h] = jnp.sum(low * grad, 0, keepdims=True) * inverse
        ga_n[:, queries_of(h)] = (grad * inverse).astype(BF16)
        att_s[:, features_of(h)] = out_t.T.astype(BF16)
        return 0

    lax.fori_loop(0, HEADS, value_head, 0, unroll=4)

    def reduce_start(kv, grad, g_ref, rg):
        g_ref[...] = grad.astype(BF16).reshape(4, Z, 16, HEAD)
        rg[z] = g_ref[:, z]
        for d in range(1, Z):
            send(g_ref.at[:, lax.rem(z + d, Z)], rg.at[z], zs.at[3, kv], zr.at[3, kv], at_z(d))

    stores = []

    def store(src, dst, i):
        stores.append(pltpu.make_async_copy(src, dst, loc.at[i]))
        stores[-1].start()

    def score_grads(rows, values):
        def head(h, _):
            grad_p = dot(values, ga_n[:, queries_of(h)])
            probs = pt_s[rows, queries_of(h)].astype(F32)
            ds_s[rows, queries_of(h)] = (probs * (grad_p - delta_s[h])).astype(BF16)
            return 0

        lax.fori_loop(0, HEADS, head, 0, unroll=4)

    prompt, own = slice(0, PROMPT), slice(PROMPT, KEYS)

    def value_grads(rows):
        return dot(pt_s[rows], ga_n[...], NT)

    def key_grads(rows):
        return dot(ds_s[rows], q3[...].reshape(HEADS * ROWS, HEAD)) * SCALE

    def query_head(h, _):
        dq = dot(kt_s[...], ds_s[:, queries_of(h)])
        gq_s[:, features_of(h)] = (dq.T * SCALE).astype(BF16)
        return 0

    def reduce_z(kv, rg, qs, rq):
        arrived(rg.at[pl.ds(0, Z - 1)], zr.at[3, kv])

        def slot(j, _):
            s = own_s[j]
            group, piece = s // 4, s % 4
            total = jnp.zeros((16, HEAD), F32)
            for source in range(Z):
                hit = jnp.full((16, HEAD), grp_s[y * Z + source], jnp.int32) == group
                total += jnp.where(hit, rg[source, piece].astype(F32), 0.0)
            qs[j] = total.astype(BF16)
            return 0

        lax.fori_loop(0, Y * Z, slot, 0, unroll=4)
        rq[y] = qs[pl.ds(y * Z, Z)]
        for d in range(1, Y):
            block = qs.at[pl.ds(lax.rem(y + d, Y) * Z, Z)]
            send(block, rq.at[y], zs.at[4, kv], zr.at[4, kv], at_y(d))

    def reduce_y(kv, rq, u, out):
        arrived(rq.at[pl.ds(0, Y - 1)], zr.at[4, kv])
        total = rq[0].astype(F32)
        for source in range(1, Y):
            total += rq[source].astype(F32)
        u[...] = total.astype(BF16)
        for d in range(1, Z):
            send(u.at[lax.rem(z + d, Z)], out.at[z], zs.at[5, kv], zr.at[5, kv], at_z(d))
        store(u.at[z], out.at[z], 10 + kv)

    core = [None] * CH
    one = [None] * CH
    two = [None] * CH

    def product(n):
        half = CW // 2

        def step(i, _):
            cols = pl.ds(pl.multiple_of(n * CW + i * half, 128), half)
            part = dot(att_s[...], w_s[:, cols]).astype(BF16)
            pb[n, :, :, :, pl.ds(pl.multiple_of(i * half, 128), half)] = part.reshape(X, 2, 32, half)
            return 0

        lax.fori_loop(0, 2, step, 0)
        core[n] = send(pb.at[n, :, 1 - c], rb1.at[n], cs.at[0], cr.at[n], partner)

    def ring_one(n):
        core[n].wait_recv()
        for d in range(X):
            b = lax.rem(x + d, X)
            acc[n, d] = (pb[n, b, c].astype(F32) + rb1[n, b].astype(F32)).astype(BF16)
        one[n] = (
            send(acc.at[n, 2, pl.ds(0, 16)], rs1.at[n, 0], r1s.at[0], r1r.at[n, 0], to_right),
            send(acc.at[n, 2, pl.ds(16, 16)], rs1.at[n, 1], r1s.at[0], r1r.at[n, 1], to_left),
        )

    def ring_two(n):
        one[n][0].wait_recv()
        acc[n, 1, :16] = (acc[n, 1, :16].astype(F32) + rs1[n, 0].astype(F32)).astype(BF16)
        first = send(acc.at[n, 1], rs2.at[n, 0], r2s.at[0], r2r.at[n, 0], to_right)
        one[n][1].wait_recv()
        acc[n, 3, 16:] = (acc[n, 3, 16:].astype(F32) + rs1[n, 1].astype(F32)).astype(BF16)
        two[n] = (
            first,
            send(acc.at[n, 3], rs2.at[n, 1], r2s.at[0], r2r.at[n, 1], to_left),
        )

    def ring_end(n):
        two[n][0].wait_recv()
        two[n][1].wait_recv()
        total = acc[n, 0].astype(F32) + rs2[n, 0].astype(F32) + rs2[n, 1].astype(F32)
        cols = pl.ds(n * CW, CW)
        bo_s[:, cols] = total.astype(BF16)
        store(bo_s.at[:, cols], bo_h.at[:, cols], 12 + n)

    reduce_start(1, value_grads(prompt), g_v, rg_v)
    score_grads(prompt, vall[:4].reshape(PROMPT, HEAD))
    reduce_start(0, key_grads(prompt), g_k, rg_k)
    product(0)
    product(1)
    ring_one(0)
    product(2)
    ring_one(1)
    product(3)
    ring_one(2)
    score_grads(own, vall[4:].reshape(ROWS, HEAD))
    reduce_z(1, rg_v, qs_v, rq_v)
    ring_one(3)
    ring_two(0)
    reduce_z(0, rg_k, qs_k, rq_k)
    kt_s[...] = kall[...].reshape(KEYS, HEAD).T
    ring_two(1)
    gkv_s[0] = key_grads(own).astype(BF16)
    store(gkv_s.at[0], gk_h, 8)
    ring_two(2)
    gkv_s[1] = value_grads(own).astype(BF16)
    store(gkv_s.at[1], gv_h, 7)
    lax.fori_loop(0, HEADS, query_head, 0, unroll=4)
    store(gq_s, gq_h, 9)
    ring_two(3)
    reduce_y(1, rq_v, u_v, gpv_h)
    reduce_y(0, rq_k, u_k, gpk_h)
    ring_end(0)
    ring_end(1)
    for kv in range(2):
        left_here(parts_k.at[pl.ds(0, Z - 1)], zs.at[0, kv])
        left_here(parts_k.at[pl.ds(0, (Y - 1) * Z)], zs.at[1, kv])
        left_here(pick_k.at[pl.ds(0, Z - 1)], zs.at[2, kv])
        left_here(rg_k.at[pl.ds(0, Z - 1)], zs.at[3, kv])
        left_here(rq_k.at[pl.ds(0, Y - 1)], zs.at[4, kv])
    left_here(cot_s.at[pl.ds(0, 3), :, pl.ds(0, BLK)], xs.at[0])
    left_here(cot_s.at[:, :, pl.ds(0, BLK)], ps.at[0])
    left_here(rb1, cs.at[0])
    left_here(rs1, r1s.at[0])
    ring_end(2)
    ring_end(3)
    left_here(rs2, r2s.at[0])
    for kv, (u, out) in ((1, (u_v, gpv_h)), (0, (u_k, gpk_h))):
        arrived(out.at[pl.ds(0, Z - 1)], zr.at[5, kv])
        left_here(u.at[pl.ds(0, Z - 1)], zs.at[5, kv])
    for cp in stores:
        cp.wait()


def place(*refs):
    ins, outs, held, wide = refs[:6], refs[6:12], refs[12:18], refs[18:20]
    taken, given = refs[20:]
    loads = [pltpu.make_async_copy(a, b, taken.at[i]) for i, (a, b) in enumerate(zip(ins, held))]
    ready = held[:4] + wide
    stores = [pltpu.make_async_copy(a, b, given.at[i]) for i, (a, b) in enumerate(zip(ready, outs))]
    for cp in loads:
        cp.start()
    for i, (load, store) in enumerate(zip(loads, stores)):
        load.wait()
        if i >= 4:
            wide[i - 4][...] = held[i][...].astype(F32)
        store.start()
    for cp in stores:
        cp.wait()


def local(
    queries, keys, values, prompt_keys, prompt_values,
    lengths, owner_slice, device_group, out_weight, cotangent,
):
    smem = pl.BlockSpec(memory_space=pltpu.SMEM)
    hbm = pl.BlockSpec(memory_space=pl.ANY)
    vm = pltpu.VMEM
    dma = pltpu.SemaphoreType.DMA
    tile = (16, HEAD)
    scratch = [
        vm((Z,) + tile, BF16),
        vm((Z,) + tile, BF16),
        vm((HEADS * HEAD, D), BF16),
        vm((X, ROWS, PAIR), BF16),
        vm((HEADS * HEAD, ROWS), F32),
        vm((HEADS, HEAD, ROWS), BF16),
        vm((ROWS, HEADS * HEAD), BF16),
        vm((HEADS, ROWS, HEAD), BF16),
        vm((6, Z) + tile, BF16),
        vm((6, Z) + tile, BF16),
        vm((HEAD, KEYS), BF16),
        vm((HEAD, KEYS), BF16),
        vm((Y * Z,) + tile, BF16),
        vm((Y * Z,) + tile, BF16),
        vm((Z, 4) + tile, BF16),
        vm((Z, 4) + tile, BF16),
        vm((ROWS, ROWS), jnp.int32),
        vm((KEYS, HEADS * ROWS), BF16),
        vm((KEYS, HEADS * ROWS), BF16),
        vm((HEAD, HEADS * ROWS), BF16),
        vm((HEADS, 1, ROWS), F32),
        vm((HEADS, 1, ROWS), F32),
        vm((ROWS, HEADS * HEAD), BF16),
        vm((ROWS, HEADS * HEAD), BF16),
        vm((2, ROWS, HEAD), BF16),
        vm((4, Z) + tile, BF16),
        vm((4, Z) + tile, BF16),
        vm((Z, 4) + tile, BF16),
        vm((Z, 4) + tile, BF16),
        vm((Y * Z,) + tile, BF16),
        vm((Y * Z,) + tile, BF16),
        vm((Y, Z) + tile, BF16),
        vm((Y, Z) + tile, BF16),
        vm((Z,) + tile, BF16),
        vm((Z,) + tile, BF16),
        vm((HEADS, ROWS, ROWS), F32),
        vm((HEADS, 1, ROWS), F32),
        vm((CH, X, 2, 32, CW), BF16),
        vm((CH, X, 32, CW), BF16),
        vm((CH, X, 32, CW), BF16),
        vm((CH, 2, 16, CW), BF16),
        vm((CH, 2, 32, CW), BF16),
        vm((32, D), BF16),
        pltpu.SMEM((Y * Z,), jnp.int32),
        dma((16,)),
        dma((6, 2)), dma((6, 2)),
        dma((1,)), dma((6,)),
        dma((1,)), dma((7,)),
        dma((1,)), dma((CH,)),
        dma((1,)), dma((CH, 2)),
        dma((1,)), dma((CH, 2)),
    ]
    shape = jax.ShapeDtypeStruct
    outs = pl.pallas_call(
        kernel,
        out_shape=(
            shape((32, D), BF16),
            shape((ROWS, HEADS * HEAD), BF16),
            shape((ROWS, HEAD), BF16),
            shape((ROWS, HEAD), BF16),
            shape((Z,) + tile, BF16),
            shape((Z,) + tile, BF16),
        ),
        in_specs=[smem] * 3 + [hbm] * 7,
        out_specs=[hbm] * 6,
        scratch_shapes=scratch,
        compiler_params=pltpu.CompilerParams(
            collective_id=0, has_side_effects=True, vmem_limit_bytes=58 * 1024 * 1024
        ),
        name="attention_block",
    )(
        lengths,
        owner_slice,
        device_group,
        queries,
        keys.reshape(2, Z, 16, HEAD),
        values.reshape(2, Z, 16, HEAD),
        prompt_keys.reshape(Z, 16, HEAD),
        prompt_values.reshape(Z, 16, HEAD),
        out_weight,
        cotangent,
    )
    wide = shape((Z,) + tile, F32)
    outs = pl.pallas_call(
        place,
        out_shape=tuple(shape(o.shape, o.dtype) for o in outs[:4]) + (wide, wide),
        in_specs=[hbm] * 6,
        out_specs=[hbm] * 6,
        scratch_shapes=[vm(o.shape, o.dtype) for o in outs]
        + [vm(wide.shape, F32)] * 2
        + [dma((6,)), dma((6,))],
        name="place",
    )(*outs)
    return outs[:4] + (outs[4].reshape(128, HEAD), outs[5].reshape(128, HEAD))


def solution(mesh):
    placed = (
        P("dp", "tensor"),
        P("dp", "tensor"),
        P("dp", "tensor"),
        P("dp", "tensor"),
        P("dp", "tensor"),
        P("dp", None),
        P(),
        P(),
        P("tensor", None),
        P("dp", "tensor"),
    )
    return jax.shard_map(
        local,
        mesh=mesh,
        in_specs=placed,
        out_specs=(
            P(("dp", "tensor"), None),
            P("dp", "tensor"),
            P("dp", "tensor"),
            P("dp", "tensor"),
            P("dp", "tensor"),
            P("dp", "tensor"),
        ),
        check_vma=False,
    )
```

```python
import functools

import jax
import jax.numpy as jnp
from jax import lax
from jax.experimental import pallas as pl
from jax.experimental.pallas import tpu as pltpu
from jax.sharding import PartitionSpec as P

Y, Z, X = 4, 8, 4
HEAD = 128
HEADS = 8
ROWS = 256
PROMPT = 512
KEYS = PROMPT + ROWS
D = 5120
BLK = D // 8
PAIR = 2 * BLK
CH = 4
CW = D // CH
SCALE = HEAD**-0.5
EXP_SCALE = SCALE * 1.4426950408889634
MASKED = -1e30 / SCALE
MESH = pl.DeviceIdType.MESH
F32, BF16 = jnp.float32, jnp.bfloat16
NT = (((1,), (1,)), ((), ()))
NN = (((1,), (0,)), ((), ()))


def dot(a, b, dims=NN):
    return lax.dot_general(a, b, dims, preferred_element_type=F32)


def kernel(
    len_s, own_s, grp_s,
    q_h, k_h, v_h, pk_h, pv_h, w_h, cot_h,
    bo_h, gq_h, gk_h, gv_h, gpk_h, gpv_h,
    pk_s, pv_s, w_s, cot_s, ga_acc, ga_t, q_s, q3, kall, vall, kt_s, vt_s, parts_k, parts_v, pick_k, pick_v,
    mask_s, pt_s, ds_s, ga_n, inverse_s, delta_s, att_s, gq_s, gkv_s,
    g_k, g_v, rg_k, rg_v, qs_k, qs_v, rq_k, rq_v, u_k, u_v, so_s, top_s,
    pb, rb1, acc, rs1, rs2, bo_s, inv_s,
    loc, zs, zr, xs, xr, ps, pr, cs, cr, r1s, r1r, r2s, r2r,
):
    me = lax.axis_index("dp")
    t = lax.axis_index("tensor")
    y, z = me // Z, me % Z
    x, c = t // 2, t % 2
    right = lax.rem(x + 1, X)
    left = lax.rem(x + X - 1, X)
    opp = lax.rem(x + 2, X)

    def at_z(d):
        return (y * Z + lax.rem(z + d, Z), t)

    def at_y(d):
        return (lax.rem(y + d, Y) * Z + z, t)

    to_right = (me, right * 2 + c)
    to_left = (me, left * 2 + c)
    partner = (me, x * 2 + 1 - c)

    def send(src, dst, ss, rs, dev):
        cp = pltpu.make_async_remote_copy(
            src_ref=src, dst_ref=dst, send_sem=ss, recv_sem=rs, device_id=dev, device_id_type=MESH
        )
        cp.start()
        return cp

    def arrived(ref, rs):
        pltpu.make_async_remote_copy(
            src_ref=ref, dst_ref=ref, send_sem=rs, recv_sem=rs, device_id=partner,
            device_id_type=MESH,
        ).wait_recv()

    def left_here(ref, ss):
        pltpu.make_async_remote_copy(
            src_ref=ref, dst_ref=ref, send_sem=ss, recv_sem=ss, device_id=partner,
            device_id_type=MESH,
        ).wait_send()

    barrier = pltpu.get_barrier_semaphore()
    peers = [at_z(d) for d in range(1, Z)] + [at_y(d) for d in range(1, Y)]
    peers += [to_right, to_left, partner]
    for dev in peers:
        pl.semaphore_signal(barrier, inc=1, device_id=dev, device_id_type=MESH)
    lane = pl.ds(pl.multiple_of(c * BLK, 128), BLK)
    loads = [
        pltpu.make_async_copy(pk_h, pk_s, loc.at[3]),
        pltpu.make_async_copy(pv_h, pv_s, loc.at[4]),
        pltpu.make_async_copy(cot_h, cot_s.at[x, :, lane], loc.at[0]),
        pltpu.make_async_copy(k_h, kall.at[pl.ds(4, 2)], loc.at[1]),
        pltpu.make_async_copy(v_h, vall.at[pl.ds(4, 2)], loc.at[2]),
        pltpu.make_async_copy(q_h, q_s, loc.at[6]),
        pltpu.make_async_copy(w_h, w_s, loc.at[5]),
    ]
    for cp in loads[:3]:
        cp.start()

    pl.semaphore_wait(barrier, len(peers))

    for kv, (src, dst) in enumerate(((pk_s, parts_k), (pv_s, parts_v))):
        loads[kv].wait()
        for d in range(1, Z):
            send(src.at[lax.rem(z + d, Z)], dst.at[me], zs.at[0, kv], zr.at[0, kv], at_z(d))
    lo, hi = pl.ds(0, 128), pl.ds(128, 128)
    own_cot = cot_s.at[x]
    loads[2].wait()

    def ring(rows, i, dev):
        ref = own_cot.at[rows, lane]
        return send(ref, ref, xs.at[0], xr.at[i], dev)

    ra = ring(lo, 0, to_right)
    lb = ring(hi, 1, to_left)
    rb = ring(hi, 2, to_right)
    la = ring(lo, 3, to_left)
    p_own = send(own_cot.at[:, lane], own_cot.at[:, lane], ps.at[0], pr.at[0], partner)
    for cp in loads[3:]:
        cp.start()
    parts_k[me] = pk_s[z]
    parts_v[me] = pv_s[z]

    def find(s, _):
        def scan(j, found):
            return jnp.where(own_s[j] == s, j, found)

        inv_s[s] = lax.fori_loop(0, Y * Z, scan, jnp.int32(0), unroll=True)
        return 0

    lax.fori_loop(0, Y * Z, find, 0)

    key_at = lax.broadcasted_iota(jnp.int32, (ROWS, ROWS), 0)
    query_at = lax.broadcasted_iota(jnp.int32, (ROWS, ROWS), 1)
    end0 = len_s[0, 0]
    end1 = end0 + len_s[0, 1]
    end2 = end1 + len_s[0, 2]

    def segment(at):
        return (
            (at >= end0).astype(jnp.int32)
            + (at >= end1).astype(jnp.int32)
            + (at >= end2).astype(jnp.int32)
        )

    seen = (segment(key_at) == segment(query_at)) & (key_at <= query_at)
    mask_s[...] = seen.astype(jnp.int32)

    def forward(block, rows, s):
        ref = cot_s.at[block, rows, lane]
        return send(ref, ref, ps.at[0], pr.at[s], partner)

    def grad_att(block, first=False, last=False):
        cols = pl.ds(pl.multiple_of(block * PAIR, 128), PAIR)

        def step(i, _):
            rows = pl.ds(pl.multiple_of(i * 512, 512), 512)
            part = dot(w_s[rows, cols], cot_s[block], NT)
            if first:
                ga_acc[rows, :] = part
            elif last:
                ga_t[pl.ds(i * 4, 4)] = (
                    (ga_acc[rows, :] + part).astype(BF16).reshape(HEADS // 2, HEAD, ROWS)
                )
            else:
                ga_acc[rows, :] += part
            return 0

        lax.fori_loop(0, 2, step, 0)

    for kv, ref in enumerate((parts_k, parts_v)):
        arrived(ref.at[pl.ds(0, Z - 1)], zr.at[0, kv])
        rows = ref.at[pl.ds(y * Z, Z)]
        for d in range(1, Y):
            send(rows, rows, zs.at[1, kv], zr.at[1, kv], at_y(d))

    ra.wait_recv()
    ref = cot_s.at[left, lo, lane]
    fr = send(ref, ref, xs.at[0], xr.at[4], to_right)
    lb.wait_recv()
    ref = cot_s.at[right, hi, lane]
    fl = send(ref, ref, xs.at[0], xr.at[5], to_left)
    p_la = forward(left, lo, 1)
    p_rb = forward(right, hi, 2)

    loads[6].wait()
    p_own.wait_recv()
    grad_att(x, first=True)

    for kv, (ref, pick, full) in enumerate(((parts_k, pick_k, kall), (parts_v, pick_v, vall))):
        arrived(ref.at[pl.ds(0, (Y - 1) * Z)], zr.at[1, kv])

        def choose(dest, _, ref=ref, pick=pick):
            first = grp_s[y * Z + dest] * 4
            for p in range(4):
                pick[dest, p] = ref[inv_s[first + p]]
            return 0

        lax.fori_loop(0, Z, choose, 0, unroll=4)
        for d in range(1, Z):
            dest = lax.rem(z + d, Z)
            send(pick.at[dest], full.at[pl.ds(0, 4), z], zs.at[2, kv], zr.at[2, kv], at_z(d))
        for p in range(4):
            full[p, z] = pick[z, p]

    for cp in loads[3:6]:
        cp.wait()
    for h in range(HEADS):
        q3[h] = q_s[:, h * HEAD : (h + 1) * HEAD]

    def own_head(h, _):
        own = dot(kall[4:].reshape(ROWS, HEAD), q3[h], NT)
        own = jnp.where(mask_s[...] != 0, own, MASKED)
        so_s[h] = own
        top_s[h] = jnp.max(own, 0, keepdims=True)
        return 0

    lax.fori_loop(0, HEADS, own_head, 0, unroll=4)
    rb.wait_recv()
    p_lb = forward(left, hi, 3)
    la.wait_recv()
    p_ra = forward(right, lo, 4)
    p_la.wait_recv()
    p_lb.wait_recv()
    grad_att(left)
    fr.wait_recv()
    p_oa = forward(opp, lo, 5)
    fl.wait_recv()
    p_ob = forward(opp, hi, 6)
    p_rb.wait_recv()
    p_ra.wait_recv()
    grad_att(right)
    def queries_of(h):
        return pl.ds(pl.multiple_of(h * ROWS, ROWS), ROWS)

    def features_of(h):
        return pl.ds(pl.multiple_of(h * HEAD, HEAD), HEAD)

    arrived(kall.at[pl.ds(0, 4), pl.ds(0, Z - 1)], zr.at[2, 0])

    def score_head(h, _):
        s0 = dot(kall[:4].reshape(PROMPT, HEAD), q3[h], NT)
        top = jnp.maximum(jnp.max(s0, 0, keepdims=True), top_s[h])
        e0 = jnp.exp2((s0 - top) * EXP_SCALE)
        e1 = jnp.exp2((so_s[h] - top) * EXP_SCALE)
        total = jnp.sum(e0, 0, keepdims=True) + jnp.sum(e1, 0, keepdims=True)
        inverse_s[h] = 1.0 / total
        pt_s[:PROMPT, queries_of(h)] = e0.astype(BF16)
        pt_s[PROMPT:, queries_of(h)] = e1.astype(BF16)
        return 0

    lax.fori_loop(0, HEADS, score_head, 0, unroll=True)

    p_oa.wait_recv()
    p_ob.wait_recv()
    grad_att(opp, last=True)

    arrived(vall.at[pl.ds(0, 4), pl.ds(0, Z - 1)], zr.at[2, 1])
    vt_s[...] = vall[...].reshape(KEYS, HEAD).T

    def value_head(h, _):
        inverse = inverse_s[h]
        out_t = dot(vt_s[...], pt_s[:, queries_of(h)]) * inverse
        low = out_t.astype(BF16).astype(F32)
        grad = ga_t[h].astype(F32)
        delta_s[h] = jnp.sum(low * grad, 0, keepdims=True) * inverse
        ga_n[:, queries_of(h)] = (grad * inverse).astype(BF16)
        att_s[:, features_of(h)] = out_t.T.astype(BF16)
        return 0

    lax.fori_loop(0, HEADS, value_head, 0, unroll=4)

    def reduce_start(kv, grad, g_ref, rg):
        g_ref[...] = grad.astype(BF16).reshape(4, Z, 16, HEAD)
        rg[z] = g_ref[:, z]
        for d in range(1, Z):
            send(g_ref.at[:, lax.rem(z + d, Z)], rg.at[z], zs.at[3, kv], zr.at[3, kv], at_z(d))

    stores = []

    def store(src, dst, i):
        stores.append(pltpu.make_async_copy(src, dst, loc.at[i]))
        stores[-1].start()

    def score_grads(rows, values):
        def head(h, _):
            grad_p = dot(values, ga_n[:, queries_of(h)])
            probs = pt_s[rows, queries_of(h)].astype(F32)
            ds_s[rows, queries_of(h)] = (probs * (grad_p - delta_s[h])).astype(BF16)
            return 0

        lax.fori_loop(0, HEADS, head, 0, unroll=4)

    prompt, own = slice(0, PROMPT), slice(PROMPT, KEYS)

    def value_grads(rows):
        return dot(pt_s[rows], ga_n[...], NT)

    def key_grads(rows):
        return dot(ds_s[rows], q3[...].reshape(HEADS * ROWS, HEAD)) * SCALE

    def query_head(h, _):
        dq = dot(kt_s[...], ds_s[:, queries_of(h)])
        gq_s[:, features_of(h)] = (dq.T * SCALE).astype(BF16)
        return 0

    def reduce_z(kv, rg, qs, rq):
        arrived(rg.at[pl.ds(0, Z - 1)], zr.at[3, kv])

        def slot(j, _):
            s = own_s[j]
            group, piece = s // 4, s % 4
            total = jnp.zeros((16, HEAD), F32)
            for source in range(Z):
                hit = jnp.full((16, HEAD), grp_s[y * Z + source], jnp.int32) == group
                total += jnp.where(hit, rg[source, piece].astype(F32), 0.0)
            qs[j] = total.astype(BF16)
            return 0

        lax.fori_loop(0, Y * Z, slot, 0, unroll=4)
        rq[y] = qs[pl.ds(y * Z, Z)]
        for d in range(1, Y):
            block = qs.at[pl.ds(lax.rem(y + d, Y) * Z, Z)]
            send(block, rq.at[y], zs.at[4, kv], zr.at[4, kv], at_y(d))

    def reduce_y(kv, rq, u, out):
        arrived(rq.at[pl.ds(0, Y - 1)], zr.at[4, kv])
        total = rq[0].astype(F32)
        for source in range(1, Y):
            total += rq[source].astype(F32)
        u[...] = total.astype(BF16)
        for d in range(1, Z):
            send(u.at[lax.rem(z + d, Z)], out.at[z], zs.at[5, kv], zr.at[5, kv], at_z(d))
        store(u.at[z], out.at[z], 10 + kv)

    core = [None] * CH
    one = [None] * CH
    two = [None] * CH

    def product(n):
        half = CW // 2

        def step(i, _):
            cols = pl.ds(pl.multiple_of(n * CW + i * half, 128), half)
            part = dot(att_s[...], w_s[:, cols]).astype(BF16)
            pb[n, :, :, :, pl.ds(pl.multiple_of(i * half, 128), half)] = part.reshape(X, 2, 32, half)
            return 0

        lax.fori_loop(0, 2, step, 0)
        core[n] = send(pb.at[n, :, 1 - c], rb1.at[n], cs.at[0], cr.at[n], partner)

    def ring_one(n):
        core[n].wait_recv()
        for d in range(X):
            b = lax.rem(x + d, X)
            acc[n, d] = (pb[n, b, c].astype(F32) + rb1[n, b].astype(F32)).astype(BF16)
        one[n] = (
            send(acc.at[n, 2, pl.ds(0, 16)], rs1.at[n, 0], r1s.at[0], r1r.at[n, 0], to_right),
            send(acc.at[n, 2, pl.ds(16, 16)], rs1.at[n, 1], r1s.at[0], r1r.at[n, 1], to_left),
        )

    def ring_two(n):
        one[n][0].wait_recv()
        acc[n, 1, :16] = (acc[n, 1, :16].astype(F32) + rs1[n, 0].astype(F32)).astype(BF16)
        first = send(acc.at[n, 1], rs2.at[n, 0], r2s.at[0], r2r.at[n, 0], to_right)
        one[n][1].wait_recv()
        acc[n, 3, 16:] = (acc[n, 3, 16:].astype(F32) + rs1[n, 1].astype(F32)).astype(BF16)
        two[n] = (
            first,
            send(acc.at[n, 3], rs2.at[n, 1], r2s.at[0], r2r.at[n, 1], to_left),
        )

    def ring_end(n):
        two[n][0].wait_recv()
        two[n][1].wait_recv()
        total = acc[n, 0].astype(F32) + rs2[n, 0].astype(F32) + rs2[n, 1].astype(F32)
        cols = pl.ds(n * CW, CW)
        bo_s[:, cols] = total.astype(BF16)
        store(bo_s.at[:, cols], bo_h.at[:, cols], 12 + n)

    reduce_start(1, value_grads(prompt), g_v, rg_v)
    score_grads(prompt, vall[:4].reshape(PROMPT, HEAD))
    reduce_start(0, key_grads(prompt), g_k, rg_k)
    product(0)
    product(1)
    ring_one(0)
    product(2)
    ring_one(1)
    product(3)
    ring_one(2)
    score_grads(own, vall[4:].reshape(ROWS, HEAD))
    reduce_z(1, rg_v, qs_v, rq_v)
    ring_one(3)
    ring_two(0)
    reduce_z(0, rg_k, qs_k, rq_k)
    kt_s[...] = kall[...].reshape(KEYS, HEAD).T
    ring_two(1)
    gkv_s[0] = key_grads(own).astype(BF16)
    store(gkv_s.at[0], gk_h, 8)
    ring_two(2)
    gkv_s[1] = value_grads(own).astype(BF16)
    store(gkv_s.at[1], gv_h, 7)
    lax.fori_loop(0, HEADS, query_head, 0, unroll=4)
    store(gq_s, gq_h, 9)
    ring_two(3)
    reduce_y(1, rq_v, u_v, gpv_h)
    reduce_y(0, rq_k, u_k, gpk_h)
    ring_end(0)
    ring_end(1)
    for kv in range(2):
        left_here(parts_k.at[pl.ds(0, Z - 1)], zs.at[0, kv])
        left_here(parts_k.at[pl.ds(0, (Y - 1) * Z)], zs.at[1, kv])
        left_here(pick_k.at[pl.ds(0, Z - 1)], zs.at[2, kv])
        left_here(rg_k.at[pl.ds(0, Z - 1)], zs.at[3, kv])
        left_here(rq_k.at[pl.ds(0, Y - 1)], zs.at[4, kv])
    left_here(cot_s.at[pl.ds(0, 3), :, pl.ds(0, BLK)], xs.at[0])
    left_here(cot_s.at[:, :, pl.ds(0, BLK)], ps.at[0])
    left_here(rb1, cs.at[0])
    left_here(rs1, r1s.at[0])
    ring_end(2)
    ring_end(3)
    left_here(rs2, r2s.at[0])
    for kv, (u, out) in ((1, (u_v, gpv_h)), (0, (u_k, gpk_h))):
        arrived(out.at[pl.ds(0, Z - 1)], zr.at[5, kv])
        left_here(u.at[pl.ds(0, Z - 1)], zs.at[5, kv])
    for cp in stores:
        cp.wait()


def place(*refs):
    ins, outs, held, wide = refs[:6], refs[6:12], refs[12:18], refs[18:20]
    taken, given = refs[20:]
    loads = [pltpu.make_async_copy(a, b, taken.at[i]) for i, (a, b) in enumerate(zip(ins, held))]
    ready = held[:4] + wide
    stores = [pltpu.make_async_copy(a, b, given.at[i]) for i, (a, b) in enumerate(zip(ready, outs))]
    for cp in loads:
        cp.start()
    for i, (load, store) in enumerate(zip(loads, stores)):
        load.wait()
        if i >= 4:
            wide[i - 4][...] = held[i][...].astype(F32)
        store.start()
    for cp in stores:
        cp.wait()


def local(
    queries, keys, values, prompt_keys, prompt_values,
    lengths, owner_slice, device_group, out_weight, cotangent,
):
    smem = pl.BlockSpec(memory_space=pltpu.SMEM)
    hbm = pl.BlockSpec(memory_space=pl.ANY)
    vm = pltpu.VMEM
    dma = pltpu.SemaphoreType.DMA
    tile = (16, HEAD)
    scratch = [
        vm((Z,) + tile, BF16),
        vm((Z,) + tile, BF16),
        vm((HEADS * HEAD, D), BF16),
        vm((X, ROWS, PAIR), BF16),
        vm((HEADS * HEAD, ROWS), F32),
        vm((HEADS, HEAD, ROWS), BF16),
        vm((ROWS, HEADS * HEAD), BF16),
        vm((HEADS, ROWS, HEAD), BF16),
        vm((6, Z) + tile, BF16),
        vm((6, Z) + tile, BF16),
        vm((HEAD, KEYS), BF16),
        vm((HEAD, KEYS), BF16),
        vm((Y * Z,) + tile, BF16),
        vm((Y * Z,) + tile, BF16),
        vm((Z, 4) + tile, BF16),
        vm((Z, 4) + tile, BF16),
        vm((ROWS, ROWS), jnp.int32),
        vm((KEYS, HEADS * ROWS), BF16),
        vm((KEYS, HEADS * ROWS), BF16),
        vm((HEAD, HEADS * ROWS), BF16),
        vm((HEADS, 1, ROWS), F32),
        vm((HEADS, 1, ROWS), F32),
        vm((ROWS, HEADS * HEAD), BF16),
        vm((ROWS, HEADS * HEAD), BF16),
        vm((2, ROWS, HEAD), BF16),
        vm((4, Z) + tile, BF16),
        vm((4, Z) + tile, BF16),
        vm((Z, 4) + tile, BF16),
        vm((Z, 4) + tile, BF16),
        vm((Y * Z,) + tile, BF16),
        vm((Y * Z,) + tile, BF16),
        vm((Y, Z) + tile, BF16),
        vm((Y, Z) + tile, BF16),
        vm((Z,) + tile, BF16),
        vm((Z,) + tile, BF16),
        vm((HEADS, ROWS, ROWS), F32),
        vm((HEADS, 1, ROWS), F32),
        vm((CH, X, 2, 32, CW), BF16),
        vm((CH, X, 32, CW), BF16),
        vm((CH, X, 32, CW), BF16),
        vm((CH, 2, 16, CW), BF16),
        vm((CH, 2, 32, CW), BF16),
        vm((32, D), BF16),
        pltpu.SMEM((Y * Z,), jnp.int32),
        dma((16,)),
        dma((6, 2)), dma((6, 2)),
        dma((1,)), dma((6,)),
        dma((1,)), dma((7,)),
        dma((1,)), dma((CH,)),
        dma((1,)), dma((CH, 2)),
        dma((1,)), dma((CH, 2)),
    ]
    shape = jax.ShapeDtypeStruct
    outs = pl.pallas_call(
        kernel,
        out_shape=(
            shape((32, D), BF16),
            shape((ROWS, HEADS * HEAD), BF16),
            shape((ROWS, HEAD), BF16),
            shape((ROWS, HEAD), BF16),
            shape((Z,) + tile, BF16),
            shape((Z,) + tile, BF16),
        ),
        in_specs=[smem] * 3 + [hbm] * 7,
        out_specs=[hbm] * 6,
        scratch_shapes=scratch,
        compiler_params=pltpu.CompilerParams(
            collective_id=0, has_side_effects=True, vmem_limit_bytes=58 * 1024 * 1024
        ),
        name="attention_block",
    )(
        lengths,
        owner_slice,
        device_group,
        queries,
        keys.reshape(2, Z, 16, HEAD),
        values.reshape(2, Z, 16, HEAD),
        prompt_keys.reshape(Z, 16, HEAD),
        prompt_values.reshape(Z, 16, HEAD),
        out_weight,
        cotangent,
    )
    wide = shape((Z,) + tile, F32)
    outs = pl.pallas_call(
        place,
        out_shape=tuple(shape(o.shape, o.dtype) for o in outs[:4]) + (wide, wide),
        in_specs=[hbm] * 6,
        out_specs=[hbm] * 6,
        scratch_shapes=[vm(o.shape, o.dtype) for o in outs]
        + [vm(wide.shape, F32)] * 2
        + [dma((6,)), dma((6,))],
        name="place",
    )(*outs)
    return outs[:4] + (outs[4].reshape(128, HEAD), outs[5].reshape(128, HEAD))


def solution(mesh):
    placed = (
        P("dp", "tensor"),
        P("dp", "tensor"),
        P("dp", "tensor"),
        P("dp", "tensor"),
        P("dp", "tensor"),
        P("dp", None),
        P(),
        P(),
        P("tensor", None),
        P("dp", "tensor"),
    )
    return jax.shard_map(
        local,
        mesh=mesh,
        in_specs=placed,
        out_specs=(
            P(("dp", "tensor"), None),
            P("dp", "tensor"),
            P("dp", "tensor"),
            P("dp", "tensor"),
            P("dp", "tensor"),
            P("dp", "tensor"),
        ),
        check_vma=False,
    )
```
